512 devices in a mesh: seq: 32 (over x_lo, z), chan: 16 (over y, x_hi, core).
Axes of the slice: x: 4 (x_hi: 2, x_lo: 2; x = x_hi * 2 + x_lo), y: 4, z: 16, core: 2. Of those that a mesh axis runs over, the one named last changes fastest.
Arguments:
- stream_in: bfloat16 [4096, 8192], P('seq', 'chan'), may hold values from -6 to 6
- features: bfloat16 [3, 4096, 8192], P(None, 'seq', 'chan'), may hold values from -6 to 6
- conv_taps: float32 [3, 3, 8192], P(None, None, 'chan'), may hold values from -3.5 to 3.5
- decay: float32 [8192, 8], P('chan'), may hold values from 0 to 1, as said below
- residues: float32 [8192, 8], P('chan'), may hold values from -1 to 1
- state_in: float32 [8192, 8], P('chan'), may hold values from -800 to 800
- out_weight: bfloat16 [8192, 8192], P('seq', 'chan'), may hold values from -0.0625 to 0.0625
Outputs:
- block_out: bfloat16 [4096, 8192], P('seq', 'chan')
The draws below stay inside these ranges and needn't reach their ends.
Inputs may be any that keep to these rules, and one draw needn't show every extreme that they name: `decay`: every rate is positive.
All inputs are finite; a program needn't handle non-finite values.
Results may differ from the reference program's by a relative error of at most 0.0046.
Values may be sent and summed in bfloat16 or wider, within the bound.
A program may use at most 64 MiB of HBM per device.

```python
import math
import jax
import jax.numpy as jnp
from jax import lax

D = 8192
POLES = 8
TAPS = 3
TOKENS = 4096


def pole_rates(key):
    base = jax.random.fold_in(key, 101)
    share = 0.5
    pick = jax.random.uniform(jax.random.fold_in(base, 1), (D, POLES), jnp.float32)
    level = jax.random.uniform(jax.random.fold_in(base, 2), (D, POLES), jnp.float32)
    slow_low = math.log(0.1 * math.log(10.0) / TOKENS)
    slow_high = math.log(math.log(10.0) / TOKENS)
    fast_low = math.log(1.0 / 50.0)
    fast_high = math.log(1.0 / 30.0)
    slow = jnp.exp(slow_low + (slow_high - slow_low) * level)
    fast = jnp.exp(fast_low + (fast_high - fast_low) * level)
    return jnp.where(pick < share, slow, fast)


def draw_decay(key, part):
    return pole_rates(key).astype(jnp.float32)


def draw_residues(key, part):
    rates = pole_rates(key)
    normal_part = jax.random.truncated_normal(jax.random.fold_in(key, 23), -4.0, 4.0, (D, POLES), jnp.float32)
    return (normal_part * jnp.sqrt(2.0 * rates / POLES)).astype(jnp.float32)


def draw_state_in(key, part):
    rates = pole_rates(key)
    normal_part = jax.random.truncated_normal(jax.random.fold_in(key, 37), -4.0, 4.0, (D, POLES), jnp.float32)
    return (normal_part * jnp.sqrt(0.5 / rates)).astype(jnp.float32)


def levels(rng, dims, shards, smallest, top_value):
    gain, own = 1.0, jax.random.fold_in(rng, 6)
    for position, parts in shards:
        steps = jnp.exp(jax.random.uniform(jax.random.fold_in(own, position), (parts,), jnp.float32, smallest / len(shards), top_value / len(shards)))
        gain = gain * jnp.repeat(steps, dims[position] // parts).reshape([-1 if axis == position else 1 for axis in range(len(dims))])
    return gain


def centred(key, shape, spread, limit, cuts=(), kind=jnp.bfloat16):
    factor_of = levels(key, shape, cuts, -0.22, 0.18) if cuts else 1.0
    drawn = jax.random.normal(key, shape, jnp.float32) * spread * factor_of
    return jnp.minimum(jnp.maximum(drawn, -limit), limit).astype(kind)


def setup_inputs(seed: int = 0) -> dict:
    seeds = jax.random.split(jax.random.key(seed), 8)
    stream_in = centred(seeds[0], (TOKENS, D), 1.0, 6.0, ((0, 32), (1, 16)))
    features = centred(seeds[1], (3, TOKENS, D), 1.0, 6.0, ((1, 32), (2, 16)))
    conv_taps = centred(seeds[2], (3, TAPS, D), TAPS ** -0.5, 3.5, ((2, 16),), jnp.float32)
    decay = draw_decay(jax.random.fold_in(seeds[7], 71), 0)
    residues = draw_residues(jax.random.fold_in(seeds[7], 71), 0)
    state_in = draw_state_in(jax.random.fold_in(seeds[7], 71), 0)
    out_weight = centred(seeds[6], (D, D), D ** -0.5, 0.0625, ((0, 32), (1, 16)))
    return {"stream_in": stream_in, "features": features, "conv_taps": conv_taps, "decay": decay, "residues": residues, "state_in": state_in, "out_weight": out_weight}


def filter_group(pieces):
    mixed_in, rates, weights, initial = pieces
    block_len = mixed_in.shape[1]
    positions = jnp.arange(block_len).astype(jnp.float32)
    offsets = (jnp.arange(block_len)[:, None] - jnp.arange(block_len)[None, :]).astype(jnp.float32)
    lower = offsets >= 0.0
    clipped = jnp.maximum(offsets, 0.0)
    toeplitz = jnp.zeros((rates.shape[0], block_len, block_len), jnp.float32)
    for pole in range(rates.shape[1]):
        term = weights[:, pole, None, None] * jnp.exp(-rates[:, pole, None, None] * clipped[None])
        toeplitz = toeplitz + jnp.where(lower[None], term, 0.0)
    inner = jnp.einsum("gij,njg->nig", toeplitz, mixed_in, precision=lax.Precision.HIGHEST)
    carried = jnp.exp(-rates[:, :, None] * (block_len - positions))
    summary = jnp.einsum("njg,grj->ngr", mixed_in, carried, precision=lax.Precision.HIGHEST)
    step_decay = jnp.exp(-rates * block_len)

    def advance(state, term):
        return step_decay * state + term, state

    last_state, starts = lax.scan(advance, initial, summary)
    outward = weights[:, :, None] * jnp.exp(-rates[:, :, None] * positions)
    cross = jnp.einsum("ngr,gri->nig", starts, outward, precision=lax.Precision.HIGHEST)
    return inner + cross


def reference(stream_in, features, conv_taps, decay, residues, state_in, out_weight):
    feats = features.astype(jnp.float32)
    padded = jnp.pad(feats, ((0, 0), (TAPS - 1, 0), (0, 0)))
    shorted = jnp.zeros_like(feats)
    for tap in range(TAPS):
        shorted = shorted + conv_taps[:, tap, None, :] * padded[:, TAPS - 1 - tap:TAPS - 1 - tap + TOKENS, :]
    product = shorted[1] * shorted[2]
    block_len = min(128, TOKENS)
    block_count = TOKENS // block_len
    group = math.gcd(D, 512)
    group_count = D // group
    mixed_in = product.reshape(block_count, block_len, group_count, group).transpose(2, 0, 1, 3)
    filtered = lax.map(filter_group, (mixed_in, decay.reshape(group_count, group, POLES),
                                      residues.reshape(group_count, group, POLES),
                                      state_in.reshape(group_count, group, POLES)))
    filtered = filtered.transpose(1, 2, 0, 3).reshape(TOKENS, D)
    gated = (shorted[0] * filtered).astype(jnp.bfloat16)
    mixed = jnp.dot(gated, out_weight, preferred_element_type=jnp.float32)
    return (stream_in.astype(jnp.float32) + mixed).astype(jnp.bfloat16)
```

```python
import jax
import jax.numpy as jnp
from jax import lax
from jax.experimental import pallas as pl
from jax.experimental.pallas import tpu as pltpu
from jax.sharding import PartitionSpec as P

MESH = pl.DeviceIdType.MESH
F32 = jnp.float32
LANES = 128
Q = 4
POLES = 8
T = 128
SUB = 8
STEPS = T // SUB
NZ = 16
NS = 32
ROUNDS = 5


def place():
    s = lax.axis_index("seq")
    c = lax.axis_index("chan")
    return s, c, s // NZ, s % NZ, c // 4, (c // 2) % 2, c % 2


def kernel(feat, taps, dec, res, sin, stream, w, out,
           wbuf, gall, gown, fraw, fpad, tail, halo, pbuf, qbuf, ybuf, xs, gf, ibuf, rbuf, sbuf, acc, cbuf,
           ws, wr, gs, gr, fs, ks, kr, hs, cs, cr, ls):
    s, c, xlo, z, y, xhi, core = place()

    def dev(xl, zz, yy, xh, co):
        return {"seq": xl * NZ + zz, "chan": yy * 4 + xh * 2 + co}

    def remote(src, dst, ssem, rsem, to):
        return pltpu.make_async_remote_copy(
            src_ref=src, dst_ref=dst, send_sem=ssem, recv_sem=rsem, device_id=to, device_id_type=MESH)

    sibling = dev(xlo, z, y, xhi, 1 - core)
    partner = dev(1 - xlo, z, y, xhi, core)
    up = dev(xlo, (z + 1) % NZ, y, xhi, core)
    down = dev(xlo, (z + NZ - 1) % NZ, y, xhi, core)

    barrier = pltpu.get_barrier_semaphore()

    def greet(to):
        pl.semaphore_signal(barrier, inc=1, device_id=to, device_id_type=MESH)

    hops = (1, 31, 2, 30, 4, 28, 8, 24, 16)
    for d in hops:
        greet({"seq": (s + d) % NS, "chan": c})
    greet(up)
    greet(down)
    greet(sibling)
    mine = xlo * 8 + y * 2 + xhi

    def greet_plane(i, carry):
        o = (mine + i) % 16
        greet(dev(o // 8, z, (o // 2) % 4, o % 2, core))
        return carry

    lax.fori_loop(1, 16, greet_plane, 0)

    load_f = pltpu.make_async_copy(feat, fraw, ls.at[Q])
    load_f.start()
    own_w = [pltpu.make_async_copy(w.at[:, pl.ds(q * LANES, LANES)], wbuf.at[q, z], ls.at[q]) for q in range(Q)]
    for o in own_w:
        o.start()
    load_f.wait()
    for i in range(3):
        fpad[i, pl.ds(8, T), :] = fraw[i].astype(F32)
        tail[pl.ds(2 * i, 2), :] = fpad[i, pl.ds(8 + T - 2, 2), :]
    tail[pl.ds(6, 2), :] = jnp.zeros((2, Q * LANES), F32)
    for o in own_w:
        o.wait()

    pl.semaphore_wait(barrier, len(hops) + 3 + 15)

    send_halo = remote(tail, halo, hs.at[0], hs.at[1], {"seq": (s + 1) % NS, "chan": c})
    send_halo.start()

    def w_copy(way, j, q):
        block = (z + NZ - j) % NZ if way == 0 else (z + j) % NZ
        return remote(wbuf.at[q, block], wbuf.at[q, block], ws.at[way, j, q], wr.at[way, j, q], up if way == 0 else down)

    def w_arrived(way, j, q):
        block = (z + NZ - j - 1) % NZ if way == 0 else (z + j + 1) % NZ
        return remote(wbuf.at[q, block], wbuf.at[q, block], ws.at[way, j, q], wr.at[way, j, q], up if way == 0 else down)

    sent = []

    def w_send(way, j, q):
        copy = w_copy(way, j, q)
        copy.start()
        sent.append((way, j, q))

    for q in range(Q):
        w_send(0, 0, q)
        w_send(1, 0, q)

    forwards = [(j, q) for j in range(1, 8) for q in range(Q)]

    def forward(count):
        for _ in range(count):
            if not forwards:
                return
            j, q = forwards.pop(0)
            for way in (0, 1):
                w_arrived(way, j - 1, q).wait_recv()
                if j < 7 or (q < 2) == (way == 0):
                    w_send(way, j, q)

    send_halo.wait_recv()
    first = s > 0
    for i in range(3):
        fpad[i, pl.ds(6, 2), :] = jnp.where(first, halo[pl.ds(2 * i, 2), :], 0.0)

    def conv(q, carry):
        cols = pl.ds(pl.multiple_of(q * LANES, LANES), LANES)

        def short(i):
            total = taps[i, 0:1, cols] * fpad[i, pl.ds(8, T), cols]
            total = total + taps[i, 1:2, cols] * fpad[i, pl.ds(7, T), cols]
            return total + taps[i, 2:3, cols] * fpad[i, pl.ds(6, T), cols]

        pbuf[q] = short(1) * short(2)
        qbuf[q] = short(0)
        return carry

    lax.fori_loop(0, Q, conv, 0)

    row = lax.broadcasted_iota(jnp.int32, (SUB, LANES), 0)

    def inner(q, carry):
        cols = pl.ds(pl.multiple_of(q * LANES, LANES), LANES)
        rates = [jnp.broadcast_to(dec[r:r + 1, cols], (SUB, LANES)) for r in range(POLES)]
        step = [jnp.exp(-v) for v in rates]
        gain = [jnp.broadcast_to(res[r:r + 1, cols], (SUB, LANES)) for r in range(POLES)]
        x = [jnp.zeros((SUB, LANES), F32) for _ in range(POLES)]
        for j in range(STEPS):
            p = pbuf[q, pl.ds(j, SUB, stride=STEPS), :]
            x = [step[r] * x[r] + p for r in range(POLES)]
            ybuf[q, j] = sum(gain[r] * x[r] for r in range(POLES))
        for r in range(POLES):
            total = step[r] * x[r]
            for d in (1, 2, 4):
                moved = jnp.where(row >= d, pltpu.roll(total, d, 0), 0.0)
                total = total + jnp.exp(rates[r] * (-1.0 * STEPS * d)) * moved
            xs[q, r] = jnp.where(row >= 1, pltpu.roll(total, 1, 0), 0.0)
            ibuf[0, q, r:r + 1, :] = total[SUB - 1:SUB, :]
        return carry

    lax.fori_loop(0, Q, inner, 0)

    def decayed(q, blocks):
        return jnp.exp(dec[:, q * LANES:(q + 1) * LANES] * (-1.0 * T * blocks))

    for q in range(Q):
        sbuf[q] = jnp.exp(dec[:, q * LANES:(q + 1) * LANES] * (-1.0 * T * s.astype(F32))) * sin[:, q * LANES:(q + 1) * LANES]
    state_sends = []
    plan = (2, 3, 3, 5, 3)
    for k in range(ROUNDS):
        d = 1 << k
        copy = remote(ibuf.at[k], rbuf.at[k], ks.at[k], kr.at[k], {"seq": (s + d) % NS, "chan": c})
        copy.start()
        state_sends.append(copy)
        forward(plan[k])
        copy.wait_recv()
        for q in range(Q):
            got = jnp.where(s >= d, rbuf[k, q], 0.0)
            sbuf[q] = sbuf[q] + decayed(q, d - 1) * got
            if k < ROUNDS - 1:
                ibuf[k + 1, q] = ibuf[k, q] + decayed(q, d) * got

    def gate(q, carry):
        cols = pl.ds(pl.multiple_of(q * LANES, LANES), LANES)
        rates = [jnp.broadcast_to(dec[r:r + 1, cols], (SUB, LANES)) for r in range(POLES)]
        step = [jnp.exp(-v) for v in rates]
        back = row.astype(F32) * (-1.0 * STEPS)
        x = []
        for r in range(POLES):
            start = xs[q, r] + jnp.exp(rates[r] * back) * sbuf[q, r:r + 1, :]
            x.append(res[r:r + 1, cols] * start)
        for j in range(STEPS):
            total = ybuf[q, j] + sum(x)
            x = [step[r] * x[r] for r in range(POLES)]
            rows = pl.ds(j, SUB, stride=STEPS)
            gf[q, rows, :] = total * qbuf[q, rows, :]
        gown[q // 2, :, pl.ds(pl.multiple_of((q % 2) * LANES, LANES), LANES)] = gf[q].astype(jnp.bfloat16)
        return carry

    lax.fori_loop(0, Q, gate, 0)

    half = y // 2
    kblk = (y % 2) * 4 + xhi * 2 + core
    spot = gall.at[xlo, pl.ds(2 * kblk, 2)]

    def g_target(i):
        o = (y * 2 + xhi + i) % 8
        return o // 2, o % 2

    for i in range(8):
        yd, xd = g_target(i)
        if i == 0:
            here = half == xlo

            @pl.when(here)
            def _():
                pltpu.make_async_copy(gown, spot, gr.at[xlo, kblk]).start()

            @pl.when(jnp.logical_not(here))
            def _():
                remote(gown, spot, gs.at[0], gr.at[xlo, kblk], dev(half, z, yd, xd, core)).start()
        else:
            remote(gown, spot, gs.at[i], gr.at[xlo, kblk], dev(half, z, yd, xd, core)).start()

    forward(8)

    def g_slot(xl, yy, xh, co):
        k = yy * 4 + xh * 2 + co
        return gall.at[xl, pl.ds(2 * k, 2)], gr.at[xl, k]

    order = [(xl, yy, xh) for xl in range(2) for yy in range(2) for xh in range(2)]
    passed = []
    for n, (xl, yy, xh) in enumerate(order):
        slot, sem = g_slot(xl, yy, xh, core)
        copy = remote(slot, slot, fs.at[n], sem, sibling)
        copy.wait_recv()
        copy.start()
        passed.append(copy)
    for xl, yy, xh in order:
        slot, sem = g_slot(xl, yy, xh, 1 - core)
        remote(slot, slot, fs.at[0], sem, sibling).wait_recv()

    def add(q, block, fresh=False):
        lhs = gall[:, block].reshape(2 * T, 2 * LANES)
        part = jnp.dot(lhs, wbuf[q, block], preferred_element_type=F32)
        acc[q] = part if fresh else acc[q] + part

    done = 7 - (len(forwards) + Q - 1) // Q

    for q in range(Q):
        add(q, z, fresh=True)

    def bulk(i, carry):
        for block in ((z + i) % NZ, (z + NZ - i) % NZ):
            for q in range(Q):
                add(q, block)
        return carry

    lax.fori_loop(1, done + 1, bulk, 0)
    while forwards:
        j = forwards[0][0]
        forward(1 if len(forwards) % Q else Q)
        if not forwards or forwards[0][0] != j:
            for block in ((z + j) % NZ, (z + NZ - j) % NZ):
                for q in range(Q):
                    add(q, block)
    sums = []
    for q in (0, 2, 1, 3):
        w_arrived(0 if q < 2 else 1, 7, q).wait_recv()
        add(q, (z + 8) % NZ)
        copy = remote(acc.at[q, pl.ds(pl.multiple_of((1 - xlo) * T, T), T)], cbuf.at[q], cs.at[q], cr.at[q], partner)
        copy.start()
        sums.append((q, copy))
    for q, copy in sums:
        copy.wait_recv()
        cols = pl.ds(q * LANES, LANES)
        mixed = acc[q, pl.ds(pl.multiple_of(xlo * T, T), T), :] + cbuf[q]
        out[:, cols] = (stream[:, cols].astype(F32) + mixed).astype(jnp.bfloat16)

    for _, copy in sums:
        copy.wait_send()
    for copy in passed:
        copy.wait_send()
    for copy in state_sends:
        copy.wait_send()
    send_halo.wait_send()
    for way, j, q in sent:
        w_copy(way, j, q).wait_send()
    for i in range(1, 8):
        remote(gown, spot, gs.at[i], gr.at[xlo, kblk], sibling).wait_send()

    @pl.when(half != xlo)
    def _():
        remote(gown, spot, gs.at[0], gr.at[xlo, kblk], sibling).wait_send()


def shards(stream_in, features, conv_taps, decay, residues, state_in, out_weight):
    vmem = pl.BlockSpec(memory_space=pltpu.VMEM)
    hbm = pl.BlockSpec(memory_space=pl.ANY)
    D = Q * LANES
    dma = pltpu.SemaphoreType.DMA
    return pl.pallas_call(
        kernel,
        out_shape=jax.ShapeDtypeStruct((T, D), jnp.bfloat16),
        in_specs=[hbm, vmem, vmem, vmem, vmem, vmem, hbm],
        out_specs=vmem,
        scratch_shapes=[
            pltpu.VMEM((Q, NZ, 2 * LANES, LANES), jnp.bfloat16),
            pltpu.VMEM((2, NZ, T, 2 * LANES), jnp.bfloat16),
            pltpu.VMEM((2, T, 2 * LANES), jnp.bfloat16),
            pltpu.VMEM((3, T, D), jnp.bfloat16),
            pltpu.VMEM((3, T + 8, D), F32),
            pltpu.VMEM((8, D), F32),
            pltpu.VMEM((8, D), F32),
            pltpu.VMEM((Q, T, LANES), F32),
            pltpu.VMEM((Q, T, LANES), F32),
            pltpu.VMEM((Q, STEPS, SUB, LANES), F32),
            pltpu.VMEM((Q, POLES, SUB, LANES), F32),
            pltpu.VMEM((Q, T, LANES), F32),
            pltpu.VMEM((ROUNDS, Q, POLES, LANES), F32),
            pltpu.VMEM((ROUNDS, Q, POLES, LANES), F32),
            pltpu.VMEM((Q, POLES, LANES), F32),
            pltpu.VMEM((Q, 2 * T, LANES), F32),
            pltpu.VMEM((Q, T, LANES), F32),
            dma((2, 8, Q)), dma((2, 8, Q)),
            dma((8,)), dma((2, 8)), dma((8,)),
            dma((ROUNDS,)), dma((ROUNDS,)),
            dma((2,)), dma((Q,)), dma((Q,)), dma((Q + 1,)),
        ],
        compiler_params=pltpu.CompilerParams(
            collective_id=0, has_side_effects=True, vmem_limit_bytes=48 * 2**20),
    )(features, conv_taps, decay.T, residues.T, state_in.T, stream_in, out_weight)


def solution(mesh):
    return jax.shard_map(
        shards,
        mesh=mesh,
        in_specs=(
            P("seq", "chan"),
            P(None, "seq", "chan"),
            P(None, None, "chan"),
            P("chan", None),
            P("chan", None),
            P("chan", None),
            P("seq", "chan"),
        ),
        out_specs=P("seq", "chan"),
        check_vma=False,
    )
```

```python
import jax
import jax.numpy as jnp
from jax import lax
from jax.experimental import pallas as pl
from jax.experimental.pallas import tpu as pltpu
from jax.sharding import PartitionSpec as P

MESH = pl.DeviceIdType.MESH
F32 = jnp.float32
LANES = 128
Q = 4
POLES = 8
T = 128
SUB = 8
STEPS = T // SUB
NZ = 16
NS = 32
ROUNDS = ((1, 2, 3), (4, 8, 12), (16,))


def place():
    s = lax.axis_index("seq")
    c = lax.axis_index("chan")
    return s, c, s // NZ, s % NZ, c // 4, (c // 2) % 2, c % 2


def kernel(feat, taps_h, dec_h, res_h, sin_h, stream_h, w, out,
           taps, dec, res, sin, stream, wbuf, gall, gown, fraw, fpad, tail, halo, pbuf, qbuf, ybuf, xs, gf, ibuf, rbuf, sbuf, acc, cbuf,
           ws, wr, gs, gr, ys, sr, fs, ks, kr, hs, cs, cr, ls):
    s, c, xlo, z, y, xhi, core = place()

    def dev(xl, zz, yy, xh, co):
        return {"seq": xl * NZ + zz, "chan": yy * 4 + xh * 2 + co}

    def remote(src, dst, ssem, rsem, to):
        return pltpu.make_async_remote_copy(
            src_ref=src, dst_ref=dst, send_sem=ssem, recv_sem=rsem, device_id=to, device_id_type=MESH)

    sibling = dev(xlo, z, y, xhi, 1 - core)
    partner = dev(1 - xlo, z, y, xhi, core)
    up = dev(xlo, (z + 1) % NZ, y, xhi, core)
    down = dev(xlo, (z + NZ - 1) % NZ, y, xhi, core)

    barrier = pltpu.get_barrier_semaphore()

    def greet(to):
        pl.semaphore_signal(barrier, inc=1, device_id=to, device_id_type=MESH)

    hops = (1, 31, 2, 30, 3, 29, 4, 28, 8, 24, 12, 20, 16)
    for d in hops:
        greet({"seq": (s + d) % NS, "chan": c})
    greet(up)
    greet(down)
    greet(sibling)
    mine = xlo * 8 + y * 2 + xhi

    def greet_plane(i, carry):
        o = (mine + i) % 16
        greet(dev(o // 8, z, (o // 2) % 4, o % 2, core))
        return carry

    lax.fori_loop(1, 16, greet_plane, 0)

    load_f = pltpu.make_async_copy(feat, fraw, ls.at[Q])
    load_f.start()
    own_w = [pltpu.make_async_copy(w.at[:, pl.ds(q * LANES, LANES)], wbuf.at[q, z], ls.at[q]) for q in range(Q)]
    for o in own_w:
        o.start()
    small = [pltpu.make_async_copy(a, b, ls.at[Q + 1 + n]) for n, (a, b) in enumerate(
        ((taps_h, taps), (dec_h, dec), (res_h, res), (sin_h, sin), (stream_h, stream)))]
    for o in small:
        o.start()
    load_f.wait()
    for i in range(3):
        fpad[i, pl.ds(8, T), :] = fraw[i].astype(F32)
        tail[pl.ds(2 * i, 2), :] = fpad[i, pl.ds(8 + T - 2, 2), :]
    tail[pl.ds(6, 2), :] = jnp.zeros((2, Q * LANES), F32)
    for o in own_w + small:
        o.wait()

    pl.semaphore_wait(barrier, len(hops) + 3 + 15)

    send_halo = remote(tail, halo, hs.at[0], hs.at[1], {"seq": (s + 1) % NS, "chan": c})
    send_halo.start()

    def w_copy(way, j, q):
        block = (z + NZ - j) % NZ if way == 0 else (z + j) % NZ
        return remote(wbuf.at[q, block], wbuf.at[q, block], ws.at[way, j, q], wr.at[way, j, q], up if way == 0 else down)

    def w_arrived(way, j, q):
        block = (z + NZ - j - 1) % NZ if way == 0 else (z + j + 1) % NZ
        return remote(wbuf.at[q, block], wbuf.at[q, block], ws.at[way, j, q], wr.at[way, j, q], up if way == 0 else down)

    sent = []

    def w_send(way, j, q):
        copy = w_copy(way, j, q)
        copy.start()
        sent.append((way, j, q))

    for q in range(Q):
        w_send(0, 0, q)
        w_send(1, 0, q)

    forwards = [(j, q) for j in range(1, 8) for q in range(Q)]

    def forward(count):
        for _ in range(count):
            if not forwards:
                return
            j, q = forwards.pop(0)
            for way in (0, 1):
                w_arrived(way, j - 1, q).wait_recv()
                if j < 7 or (q < 2) == (way == 0):
                    w_send(way, j, q)

    send_halo.wait_recv()
    first = s > 0
    for i in range(3):
        fpad[i, pl.ds(6, 2), :] = jnp.where(first, halo[pl.ds(2 * i, 2), :], 0.0)

    def conv(q, carry):
        cols = pl.ds(pl.multiple_of(q * LANES, LANES), LANES)

        def short(i):
            total = taps[i, 0:1, cols] * fpad[i, pl.ds(8, T), cols]
            total = total + taps[i, 1:2, cols] * fpad[i, pl.ds(7, T), cols]
            return total + taps[i, 2:3, cols] * fpad[i, pl.ds(6, T), cols]

        pbuf[q] = short(1) * short(2)
        qbuf[q] = short(0)
        return carry

    lax.fori_loop(0, Q, conv, 0)

    row = lax.broadcasted_iota(jnp.int32, (SUB, LANES), 0)

    def inner(q, carry):
        cols = pl.ds(pl.multiple_of(q * LANES, LANES), LANES)
        rates = [jnp.broadcast_to(dec[r:r + 1, cols], (SUB, LANES)) for r in range(POLES)]
        step = [jnp.exp(-v) for v in rates]
        gain = [jnp.broadcast_to(res[r:r + 1, cols], (SUB, LANES)) for r in range(POLES)]
        x = [jnp.zeros((SUB, LANES), F32) for _ in range(POLES)]
        for j in range(STEPS):
            p = pbuf[q, pl.ds(j, SUB, stride=STEPS), :]
            x = [step[r] * x[r] + p for r in range(POLES)]
            ybuf[q, j] = sum(gain[r] * x[r] for r in range(POLES))
        for r in range(POLES):
            total = step[r] * x[r]
            for d in (1, 2, 4):
                moved = jnp.where(row >= d, pltpu.roll(total, d, 0), 0.0)
                total = total + jnp.exp(rates[r] * (-1.0 * STEPS * d)) * moved
            xs[q, r] = jnp.where(row >= 1, pltpu.roll(total, 1, 0), 0.0)
            ibuf[0, q, r:r + 1, :] = total[SUB - 1:SUB, :]
        return carry

    lax.fori_loop(0, Q, inner, 0)

    def decayed(q, blocks):
        return jnp.exp(dec[:, q * LANES:(q + 1) * LANES] * (-1.0 * T * blocks))

    for q in range(Q):
        sbuf[q] = jnp.exp(dec[:, q * LANES:(q + 1) * LANES] * (-1.0 * T * s.astype(F32))) * sin[:, q * LANES:(q + 1) * LANES]
    state_sends = []
    plan = (4, 5, 3)
    slot = 0
    for k, distances in enumerate(ROUNDS):
        copies = [remote(ibuf.at[k], rbuf.at[slot + n], ks.at[slot + n], kr.at[slot + n], {"seq": (s + d) % NS, "chan": c})
                  for n, d in enumerate(distances)]
        for copy in copies:
            copy.start()
        forward(plan[k])
        for n, d in enumerate(distances):
            copies[n].wait_recv()
            for q in range(Q):
                got = jnp.where(s >= d, rbuf[slot + n, q], 0.0)
                sbuf[q] = sbuf[q] + decayed(q, d - 1) * got
                if k < len(ROUNDS) - 1:
                    before = ibuf[k, q] if n == 0 else ibuf[k + 1, q]
                    ibuf[k + 1, q] = before + decayed(q, d) * got
        slot += len(distances)
        state_sends += copies

    def gate(q, carry):
        cols = pl.ds(pl.multiple_of(q * LANES, LANES), LANES)
        rates = [jnp.broadcast_to(dec[r:r + 1, cols], (SUB, LANES)) for r in range(POLES)]
        step = [jnp.exp(-v) for v in rates]
        back = row.astype(F32) * (-1.0 * STEPS)
        x = []
        for r in range(POLES):
            start = xs[q, r] + jnp.exp(rates[r] * back) * sbuf[q, r:r + 1, :]
            x.append(res[r:r + 1, cols] * start)
        for j in range(STEPS):
            total = ybuf[q, j] + sum(x)
            x = [step[r] * x[r] for r in range(POLES)]
            rows = pl.ds(j, SUB, stride=STEPS)
            gf[q, rows, :] = total * qbuf[q, rows, :]
        gown[q // 2, :, pl.ds(pl.multiple_of((q % 2) * LANES, LANES), LANES)] = gf[q].astype(jnp.bfloat16)
        return carry

    lax.fori_loop(0, Q, gate, 0)

    def spot(yy):
        other = (yy // 2 + xlo) % 2
        k = ((yy % 2) * 4 + xhi * 2 + core) * (1 - other) + (yy % 2) * other
        return gall.at[xlo * (1 - other) + 2 * other, pl.ds(2 * k, 2)]

    def landing(yy):
        k = (yy % 2) * 4 + xhi * 2 + core
        return gall.at[xlo, pl.ds(2 * k, 2)], gr.at[xlo, k]

    def along_x(dx):
        x = (xhi * 2 + xlo + dx) % 4
        return dev(x % 2, z, y, x // 2, core)

    def send_x(n, src):
        yy = (y + n) % 4
        dst, sem = landing(yy)
        same = yy // 2 == xlo

        @pl.when(same)
        def _():
            remote(src, dst, gs.at[n, 0], sem, along_x(2)).start()

        @pl.when(jnp.logical_not(same))
        def _():
            remote(src, dst, gs.at[n, 0], sem, along_x(1)).start()
            remote(src, dst, gs.at[n, 1], sem, along_x(3)).start()

    home = y // 2 == xlo

    @pl.when(home)
    def _():
        pltpu.make_async_copy(gown, spot(y), sr.at[y]).start()

    send_x(0, gown)
    y_sends = [remote(gown, spot(y), ys.at[n], sr.at[y], dev(xlo, z, (y + n) % 4, xhi, core)) for n in (1, 2, 3)]
    for copy in y_sends:
        copy.start()
    passed = []

    def to_sibling(slot, sem):
        copy = remote(slot, slot, fs.at[len(passed)], sem, sibling)
        copy.start()
        passed.append((slot, sem))

    forward(3)
    for n in (1, 3, 2):
        yy = (y + n) % 4
        remote(spot(yy), spot(yy), ys.at[n], sr.at[yy], sibling).wait_recv()
        send_x(n, spot(yy))
        forward(1)

    def arrived(xl, yy, xh, co):
        k = yy * 4 + xh * 2 + co
        return gall.at[xl, pl.ds(2 * k, 2)], gr.at[xl, k]

    @pl.when(home)
    def _():
        pltpu.make_async_copy(gown, spot(y), sr.at[y]).wait()

    for yy in range(2):
        to_sibling(*arrived(xlo, yy, xhi, core))
    for yy in range(2):
        for xl, xh in ((1 - xlo, xhi), (1 - xlo, 1 - xhi), (xlo, 1 - xhi)):
            slot, sem = arrived(xl, yy, xh, core)
            remote(slot, slot, fs.at[0], sem, sibling).wait_recv()
            to_sibling(slot, sem)
        forward(1)
    for xl in range(2):
        for yy in range(2):
            for xh in range(2):
                slot, sem = arrived(xl, yy, xh, 1 - core)
                remote(slot, slot, fs.at[0], sem, sibling).wait_recv()

    def add(q, block, fresh=False):
        lhs = gall[pl.ds(0, 2), block].reshape(2 * T, 2 * LANES)
        part = jnp.dot(lhs, wbuf[q, block], preferred_element_type=F32)
        acc[q] = part if fresh else acc[q] + part

    done = 7 - (len(forwards) + Q - 1) // Q

    for q in range(Q):
        add(q, z, fresh=True)

    def bulk(i, carry):
        for block in ((z + i) % NZ, (z + NZ - i) % NZ):
            for q in range(Q):
                add(q, block)
        return carry

    lax.fori_loop(1, done + 1, bulk, 0)
    while forwards:
        j = forwards[0][0]
        forward(1 if len(forwards) % Q else Q)
        if not forwards or forwards[0][0] != j:
            for block in ((z + j) % NZ, (z + NZ - j) % NZ):
                for q in range(Q):
                    add(q, block)
    sums = []
    for q in (0, 2, 1, 3):
        w_arrived(0 if q < 2 else 1, 7, q).wait_recv()
        add(q, (z + 8) % NZ)
        copy = remote(acc.at[q, pl.ds(pl.multiple_of((1 - xlo) * T, T), T)], cbuf.at[q], cs.at[q], cr.at[q], partner)
        copy.start()
        sums.append((q, copy))
    for q, copy in sums:
        copy.wait_recv()
        cols = pl.ds(q * LANES, LANES)
        mixed = acc[q, pl.ds(pl.multiple_of(xlo * T, T), T), :] + cbuf[q]
        out[:, cols] = (stream[:, cols].astype(F32) + mixed).astype(jnp.bfloat16)

    for _, copy in sums:
        copy.wait_send()
    for n, (slot, sem) in enumerate(passed):
        remote(slot, slot, fs.at[n], sem, sibling).wait_send()
    for copy in state_sends:
        copy.wait_send()
    send_halo.wait_send()
    for way, j, q in sent:
        w_copy(way, j, q).wait_send()
    for copy in y_sends:
        copy.wait_send()
    for n in range(4):
        dst, sem = landing((y + n) % 4)
        remote(gown, dst, gs.at[n, 0], sem, sibling).wait_send()

        @pl.when((y + n) % 4 // 2 != xlo)
        def _():
            remote(gown, dst, gs.at[n, 1], sem, sibling).wait_send()


def shards(stream_in, features, conv_taps, decay, residues, state_in, out_weight):
    vmem = pl.BlockSpec(memory_space=pltpu.VMEM)
    hbm = pl.BlockSpec(memory_space=pl.ANY)
    D = Q * LANES
    dma = pltpu.SemaphoreType.DMA
    return pl.pallas_call(
        kernel,
        out_shape=jax.ShapeDtypeStruct((T, D), jnp.bfloat16),
        in_specs=[hbm] * 7,
        out_specs=vmem,
        scratch_shapes=[
            pltpu.VMEM((3, 3, D), F32),
            pltpu.VMEM((POLES, D), F32),
            pltpu.VMEM((POLES, D), F32),
            pltpu.VMEM((POLES, D), F32),
            pltpu.VMEM((T, D), jnp.bfloat16),
            pltpu.VMEM((Q, NZ, 2 * LANES, LANES), jnp.bfloat16),
            pltpu.VMEM((3, NZ, T, 2 * LANES), jnp.bfloat16),
            pltpu.VMEM((2, T, 2 * LANES), jnp.bfloat16),
            pltpu.VMEM((3, T, D), jnp.bfloat16),
            pltpu.VMEM((3, T + 8, D), F32),
            pltpu.VMEM((8, D), F32),
            pltpu.VMEM((8, D), F32),
            pltpu.VMEM((Q, T, LANES), F32),
            pltpu.VMEM((Q, T, LANES), F32),
            pltpu.VMEM((Q, STEPS, SUB, LANES), F32),
            pltpu.VMEM((Q, POLES, SUB, LANES), F32),
            pltpu.VMEM((Q, T, LANES), F32),
            pltpu.VMEM((len(ROUNDS), Q, POLES, LANES), F32),
            pltpu.VMEM((7, Q, POLES, LANES), F32),
            pltpu.VMEM((Q, POLES, LANES), F32),
            pltpu.VMEM((Q, 2 * T, LANES), F32),
            pltpu.VMEM((Q, T, LANES), F32),
            dma((2, 8, Q)), dma((2, 8, Q)),
            dma((4, 2)), dma((2, 8)), dma((4,)), dma((4,)), dma((8,)),
            dma((7,)), dma((7,)),
            dma((2,)), dma((Q,)), dma((Q,)), dma((Q + 6,)),
        ],
        compiler_params=pltpu.CompilerParams(
            collective_id=0, has_side_effects=True, vmem_limit_bytes=60 * 2**20),
    )(features, conv_taps, decay.T, residues.T, state_in.T, stream_in, out_weight)


def solution(mesh):
    return jax.shard_map(
        shards,
        mesh=mesh,
        in_specs=(
            P("seq", "chan"),
            P(None, "seq", "chan"),
            P(None, None, "chan"),
            P("chan", None),
            P("chan", None),
            P("chan", None),
            P("seq", "chan"),
        ),
        out_specs=P("seq", "chan"),
        check_vma=False,
    )
```

```python
import jax
import jax.numpy as jnp
from jax import lax
from jax.experimental import pallas as pl
from jax.experimental.pallas import tpu as pltpu
from jax.sharding import PartitionSpec as P

FIRST, EACH = 3.6, 1.45
STATE_AT = (10.0, 17.0, 19.5)
Y_AT = {1: 25.0, 3: 26.0, 2: 28.5}
X_AT = (29.0, 30.0, 31.0, 33.0, 35.0, 36.0)
SIBLING_AT = 37.0
DOT = 0.25

MESH = pl.DeviceIdType.MESH
F32 = jnp.float32
LANES = 128
WIDE = 256
Q = 4
POLES = 8
T = 128
SUB = 8
STEPS = T // SUB
NZ = 16
NS = 32
ROUNDS = ((1, 2, 3), (4, 8, 12), (16,))


def place():
    s = lax.axis_index("seq")
    c = lax.axis_index("chan")
    return s, c, s // NZ, s % NZ, c // 4, (c // 2) % 2, c % 2


def kernel(feat, taps_h, dec_h, res_h, sin_h, stream_h, w, out,
           taps, dec, res, sin, stream, wbuf, gall, gown, fraw, fpad, tail, halo, pbuf, qbuf, ybuf, xs, gf, ibuf, rbuf, sbuf, acc, csrc, cbuf,
           ws, wr, gs, gr, ys, sr, fs, ks, kr, hs, cs, cr, ls):
    s, c, xlo, z, y, xhi, core = place()

    def dev(xl, zz, yy, xh, co):
        return {"seq": xl * NZ + zz, "chan": yy * 4 + xh * 2 + co}

    def remote(src, dst, ssem, rsem, to):
        return pltpu.make_async_remote_copy(
            src_ref=src, dst_ref=dst, send_sem=ssem, recv_sem=rsem, device_id=to, device_id_type=MESH)

    sibling = dev(xlo, z, y, xhi, 1 - core)
    partner = dev(1 - xlo, z, y, xhi, core)
    up = dev(xlo, (z + 1) % NZ, y, xhi, core)
    down = dev(xlo, (z + NZ - 1) % NZ, y, xhi, core)

    barrier = pltpu.get_barrier_semaphore()

    def greet(to):
        pl.semaphore_signal(barrier, inc=1, device_id=to, device_id_type=MESH)

    hops = (1, 31, 2, 30, 3, 29, 4, 28, 8, 24, 12, 20, 16)
    for d in hops:
        greet({"seq": (s + d) % NS, "chan": c})
    greet(up)
    greet(down)
    greet(sibling)
    mine = xlo * 8 + y * 2 + xhi

    def greet_plane(i, carry):
        o = (mine + i) % 16
        greet(dev(o // 8, z, (o // 2) % 4, o % 2, core))
        return carry

    lax.fori_loop(1, 16, greet_plane, 0)

    load_f = pltpu.make_async_copy(feat, fraw, ls.at[Q])
    load_f.start()
    own_w = [pltpu.make_async_copy(w.at[:, pl.ds(n * WIDE, WIDE)], wbuf.at[n, z], ls.at[n]) for n in range(2)]
    for o in own_w:
        o.start()
    small = [pltpu.make_async_copy(a, b, ls.at[Q + 1 + n]) for n, (a, b) in enumerate(
        ((taps_h, taps), (dec_h, dec), (res_h, res), (sin_h, sin), (stream_h, stream)))]
    for o in small:
        o.start()
    load_f.wait()
    for i in range(3):
        fpad[i, pl.ds(8, T), :] = fraw[i].astype(F32)
        tail[pl.ds(2 * i, 2), :] = fpad[i, pl.ds(8 + T - 2, 2), :]
    tail[pl.ds(6, 2), :] = jnp.zeros((2, Q * LANES), F32)
    for o in own_w + small:
        o.wait()

    pl.semaphore_wait(barrier, len(hops) + 3 + 15)

    send_halo = remote(tail, halo, hs.at[0], hs.at[1], {"seq": (s + 1) % NS, "chan": c})
    send_halo.start()

    def chunk(block, q):
        return wbuf.at[q // 2, block, pl.ds(q % 2 * LANES, LANES)]

    def w_copy(way, j, q):
        block = (z + NZ - j) % NZ if way == 0 else (z + j) % NZ
        return remote(chunk(block, q), chunk(block, q), ws.at[way, j, q], wr.at[way, j, q], up if way == 0 else down)

    def w_arrived(way, j, q):
        block = (z + NZ - j - 1) % NZ if way == 0 else (z + j + 1) % NZ
        return remote(chunk(block, q), chunk(block, q), ws.at[way, j, q], wr.at[way, j, q], up if way == 0 else down)

    sent = []

    def w_send(way, j, q):
        copy = w_copy(way, j, q)
        copy.start()
        sent.append((way, j, q))

    for q in range(Q):
        w_send(0, 0, q)
        w_send(1, 0, q)

    forwards = [(j, q) for j in range(1, 8) for q in range(Q)]

    def until(t):
        while forwards and FIRST + EACH * (4 * (forwards[0][0] - 1) + forwards[0][1]) <= t:
            j, q = forwards.pop(0)
            for way in (0, 1):
                w_arrived(way, j - 1, q).wait_recv()
                if j < 7 or q % 2 == way:
                    w_send(way, j, q)

    send_halo.wait_recv()
    first = s > 0
    for i in range(3):
        fpad[i, pl.ds(6, 2), :] = jnp.where(first, halo[pl.ds(2 * i, 2), :], 0.0)

    def conv(q, carry):
        cols = pl.ds(pl.multiple_of(q * LANES, LANES), LANES)

        def short(i):
            total = taps[i, 0:1, cols] * fpad[i, pl.ds(8, T), cols]
            total = total + taps[i, 1:2, cols] * fpad[i, pl.ds(7, T), cols]
            return total + taps[i, 2:3, cols] * fpad[i, pl.ds(6, T), cols]

        pbuf[q] = short(1) * short(2)
        qbuf[q] = short(0)
        return carry

    lax.fori_loop(0, Q, conv, 0)

    row = lax.broadcasted_iota(jnp.int32, (SUB, LANES), 0)

    def inner(q, carry):
        cols = pl.ds(pl.multiple_of(q * LANES, LANES), LANES)
        rates = [jnp.broadcast_to(dec[r:r + 1, cols], (SUB, LANES)) for r in range(POLES)]
        step = [jnp.exp(-v) for v in rates]
        gain = [jnp.broadcast_to(res[r:r + 1, cols], (SUB, LANES)) for r in range(POLES)]
        x = [jnp.zeros((SUB, LANES), F32) for _ in range(POLES)]
        for j in range(STEPS):
            p = pbuf[q, pl.ds(j, SUB, stride=STEPS), :]
            x = [step[r] * x[r] + p for r in range(POLES)]
            ybuf[q, j] = sum(gain[r] * x[r] for r in range(POLES))
        for r in range(POLES):
            total = step[r] * x[r]
            for d in (1, 2, 4):
                moved = jnp.where(row >= d, pltpu.roll(total, d, 0), 0.0)
                total = total + jnp.exp(rates[r] * (-1.0 * STEPS * d)) * moved
            xs[q, r] = jnp.where(row >= 1, pltpu.roll(total, 1, 0), 0.0)
            ibuf[0, q, r:r + 1, :] = total[SUB - 1:SUB, :]
        return carry

    lax.fori_loop(0, Q, inner, 0)

    def decayed(q, blocks):
        return jnp.exp(dec[:, q * LANES:(q + 1) * LANES] * (-1.0 * T * blocks))

    for q in range(Q):
        sbuf[q] = jnp.exp(dec[:, q * LANES:(q + 1) * LANES] * (-1.0 * T * s.astype(F32))) * sin[:, q * LANES:(q + 1) * LANES]
    state_sends = []
    slot = 0
    for k, distances in enumerate(ROUNDS):
        copies = [remote(ibuf.at[k], rbuf.at[slot + n], ks.at[slot + n], kr.at[slot + n], {"seq": (s + d) % NS, "chan": c})
                  for n, d in enumerate(distances)]
        for copy in copies:
            copy.start()
        until(STATE_AT[k])
        for n, d in enumerate(distances):
            copies[n].wait_recv()
            for q in range(Q):
                got = jnp.where(s >= d, rbuf[slot + n, q], 0.0)
                sbuf[q] = sbuf[q] + decayed(q, d - 1) * got
                if k < len(ROUNDS) - 1:
                    before = ibuf[k, q] if n == 0 else ibuf[k + 1, q]
                    ibuf[k + 1, q] = before + decayed(q, d) * got
        slot += len(distances)
        state_sends += copies

    def gate(q, carry):
        cols = pl.ds(pl.multiple_of(q * LANES, LANES), LANES)
        rates = [jnp.broadcast_to(dec[r:r + 1, cols], (SUB, LANES)) for r in range(POLES)]
        step = [jnp.exp(-v) for v in rates]
        back = row.astype(F32) * (-1.0 * STEPS)
        x = []
        for r in range(POLES):
            start = xs[q, r] + jnp.exp(rates[r] * back) * sbuf[q, r:r + 1, :]
            x.append(res[r:r + 1, cols] * start)
        for j in range(STEPS):
            total = ybuf[q, j] + sum(x)
            x = [step[r] * x[r] for r in range(POLES)]
            rows = pl.ds(j, SUB, stride=STEPS)
            gf[q, rows, :] = total * qbuf[q, rows, :]
        gown[q // 2, :, pl.ds(pl.multiple_of((q % 2) * LANES, LANES), LANES)] = gf[q].astype(jnp.bfloat16)
        return carry

    lax.fori_loop(0, Q, gate, 0)

    def spot(yy):
        other = (yy // 2 + xlo) % 2
        k = ((yy % 2) * 4 + xhi * 2 + core) * (1 - other) + (yy % 2) * other
        return gall.at[xlo * (1 - other) + 2 * other, pl.ds(2 * k, 2)]

    def landing(yy):
        k = (yy % 2) * 4 + xhi * 2 + core
        return gall.at[xlo, pl.ds(2 * k, 2)], gr.at[xlo, k]

    def along_x(dx):
        x = (xhi * 2 + xlo + dx) % 4
        return dev(x % 2, z, y, x // 2, core)

    def send_x(n, src):
        yy = (y + n) % 4
        dst, sem = landing(yy)
        same = yy // 2 == xlo

        @pl.when(same)
        def _():
            remote(src, dst, gs.at[n, 0], sem, along_x(2)).start()

        @pl.when(jnp.logical_not(same))
        def _():
            remote(src, dst, gs.at[n, 0], sem, along_x(1)).start()
            remote(src, dst, gs.at[n, 1], sem, along_x(3)).start()

    home = y // 2 == xlo

    @pl.when(home)
    def _():
        pltpu.make_async_copy(gown, spot(y), sr.at[y]).start()

    send_x(0, gown)
    y_sends = [remote(gown, spot(y), ys.at[n], sr.at[y], dev(xlo, z, (y + n) % 4, xhi, core)) for n in (1, 2, 3)]
    for copy in y_sends:
        copy.start()
    passed = []

    def to_sibling(slot, sem):
        copy = remote(slot, slot, fs.at[len(passed)], sem, sibling)
        copy.start()
        passed.append((slot, sem))

    for n in (1, 3, 2):
        until(Y_AT[n])
        yy = (y + n) % 4
        remote(spot(yy), spot(yy), ys.at[n], sr.at[yy], sibling).wait_recv()
        send_x(n, spot(yy))

    def arrived(xl, yy, xh, co):
        k = yy * 4 + xh * 2 + co
        return gall.at[xl, pl.ds(2 * k, 2)], gr.at[xl, k]

    @pl.when(home)
    def _():
        pltpu.make_async_copy(gown, spot(y), sr.at[y]).wait()

    for yy in range(2):
        to_sibling(*arrived(xlo, yy, xhi, core))
    for yy in range(2):
        for xl, xh in ((1 - xlo, xhi), (1 - xlo, 1 - xhi), (xlo, 1 - xhi)):
            until(X_AT[len(passed) - 2])
            slot, sem = arrived(xl, yy, xh, core)
            remote(slot, slot, fs.at[0], sem, sibling).wait_recv()
            to_sibling(slot, sem)
    until(SIBLING_AT)
    for xl in range(2):
        for yy in range(2):
            for xh in range(2):
                slot, sem = arrived(xl, yy, xh, 1 - core)
                remote(slot, slot, fs.at[0], sem, sibling).wait_recv()

    def add(n, block, fresh=False):
        lhs = gall[pl.ds(0, 2), block].reshape(2 * T, WIDE)
        part = jnp.dot(lhs, wbuf[n, block], preferred_element_type=F32)
        acc[n] = part if fresh else acc[n] + part

    clock = SIBLING_AT
    for n in range(2):
        add(n, z, fresh=True)
    for i in range(1, 8):
        for block in ((z + i) % NZ, (z + NZ - i) % NZ):
            clock += DOT
            until(clock)
            while forwards and forwards[0][0] <= i:
                until(FIRST + EACH * (4 * (forwards[0][0] - 1) + forwards[0][1]))
            for n in range(2):
                add(n, block)
    sums = []
    for n in range(2):
        for way in (0, 1):
            w_arrived(way, 7, 2 * n + way).wait_recv()
        add(n, (z + 8) % NZ)
        csrc[n] = acc[n, pl.ds(pl.multiple_of((1 - xlo) * T, T), T), :].astype(jnp.bfloat16)
        copy = remote(csrc.at[n], cbuf.at[n], cs.at[n], cr.at[n], partner)
        copy.start()
        sums.append(copy)
    for n, copy in enumerate(sums):
        copy.wait_recv()
        cols = pl.ds(n * WIDE, WIDE)
        mixed = acc[n, pl.ds(pl.multiple_of(xlo * T, T), T), :] + cbuf[n].astype(F32)
        out[:, cols] = (stream[:, cols].astype(F32) + mixed).astype(jnp.bfloat16)

    for copy in sums:
        copy.wait_send()
    for n, (slot, sem) in enumerate(passed):
        remote(slot, slot, fs.at[n], sem, sibling).wait_send()
    for copy in state_sends:
        copy.wait_send()
    send_halo.wait_send()
    for way, j, q in sent:
        w_copy(way, j, q).wait_send()
    for copy in y_sends:
        copy.wait_send()
    for n in range(4):
        dst, sem = landing((y + n) % 4)
        remote(gown, dst, gs.at[n, 0], sem, sibling).wait_send()

        @pl.when((y + n) % 4 // 2 != xlo)
        def _():
            remote(gown, dst, gs.at[n, 1], sem, sibling).wait_send()


def shards(stream_in, features, conv_taps, decay, residues, state_in, out_weight):
    vmem = pl.BlockSpec(memory_space=pltpu.VMEM)
    hbm = pl.BlockSpec(memory_space=pl.ANY)
    D = Q * LANES
    dma = pltpu.SemaphoreType.DMA
    return pl.pallas_call(
        kernel,
        out_shape=jax.ShapeDtypeStruct((T, D), jnp.bfloat16),
        in_specs=[hbm] * 7,
        out_specs=vmem,
        scratch_shapes=[
            pltpu.VMEM((3, 3, D), F32),
            pltpu.VMEM((POLES, D), F32),
            pltpu.VMEM((POLES, D), F32),
            pltpu.VMEM((POLES, D), F32),
            pltpu.VMEM((T, D), jnp.bfloat16),
            pltpu.VMEM((2, NZ, WIDE, WIDE), jnp.bfloat16),
            pltpu.VMEM((3, NZ, T, 2 * LANES), jnp.bfloat16),
            pltpu.VMEM((2, T, 2 * LANES), jnp.bfloat16),
            pltpu.VMEM((3, T, D), jnp.bfloat16),
            pltpu.VMEM((3, T + 8, D), F32),
            pltpu.VMEM((8, D), F32),
            pltpu.VMEM((8, D), F32),
            pltpu.VMEM((Q, T, LANES), F32),
            pltpu.VMEM((Q, T, LANES), F32),
            pltpu.VMEM((Q, STEPS, SUB, LANES), F32),
            pltpu.VMEM((Q, POLES, SUB, LANES), F32),
            pltpu.VMEM((Q, T, LANES), F32),
            pltpu.VMEM((len(ROUNDS), Q, POLES, LANES), F32),
            pltpu.VMEM((7, Q, POLES, LANES), F32),
            pltpu.VMEM((Q, POLES, LANES), F32),
            pltpu.VMEM((2, 2 * T, WIDE), F32),
            pltpu.VMEM((2, T, WIDE), jnp.bfloat16),
            pltpu.VMEM((2, T, WIDE), jnp.bfloat16),
            dma((2, 8, Q)), dma((2, 8, Q)),
            dma((4, 2)), dma((2, 8)), dma((4,)), dma((4,)), dma((8,)),
            dma((7,)), dma((7,)),
            dma((2,)), dma((2,)), dma((2,)), dma((Q + 6,)),
        ],
        compiler_params=pltpu.CompilerParams(
            collective_id=0, has_side_effects=True, vmem_limit_bytes=60 * 2**20),
    )(features, conv_taps, decay.T, residues.T, state_in.T, stream_in, out_weight)


def solution(mesh):
    return jax.shard_map(
        shards,
        mesh=mesh,
        in_specs=(
            P("seq", "chan"),
            P(None, "seq", "chan"),
            P(None, None, "chan"),
            P("chan", None),
            P("chan", None),
            P("chan", None),
            P("seq", "chan"),
        ),
        out_specs=P("seq", "chan"),
        check_vma=False,
    )
```

```python
import jax
import jax.numpy as jnp
from jax import lax
from jax.experimental import pallas as pl
from jax.experimental.pallas import tpu as pltpu
from jax.sharding import PartitionSpec as P

FIRST, EACH = 3.6, 1.45
KNOW_AT = (2.5, 5.5, 9.5)
ENDS_AT, TOTAL_AT, STARTS_AT = 15.0, 18.0, 23.5
Y_AT = {1: 28.5, 3: 29.5, 2: 31.5}
X_AT = (32.0, 33.0, 34.0, 36.0, 38.0, 39.0)
SIBLING_AT = 40.0
DOT = 0.25

MESH = pl.DeviceIdType.MESH
F32 = jnp.float32
LANES = 128
WIDE = 256
Q = 4
POLES = 8
T = 128
SUB = 8
STEPS = T // SUB
NZ = 16
NS = 32


def place():
    s = lax.axis_index("seq")
    c = lax.axis_index("chan")
    return s, c, s // NZ, s % NZ, c // 4, (c // 2) % 2, c % 2


def kernel(feat, taps_h, dec_h, res_h, sin_h, stream_h, w, out,
           taps, dec, res, sin, stream, wbuf, gall, gown, fraw, fpad, tail, halo, pbuf, qbuf, ybuf, xs, gf, ends, ends_in, starts, starts_in, dec16, sin16, seed, total_out, total_in, sbuf, acc, csrc, cbuf,
           ws, wr, gs, gr, ys, sr, fs, es, er, ts, tr, ps, hs, cs, cr, ls, know):
    s, c, xlo, z, y, xhi, core = place()

    def dev(xl, zz, yy, xh, co):
        return {"seq": xl * NZ + zz, "chan": yy * 4 + xh * 2 + co}

    def remote(src, dst, ssem, rsem, to):
        return pltpu.make_async_remote_copy(
            src_ref=src, dst_ref=dst, send_sem=ssem, recv_sem=rsem, device_id=to, device_id_type=MESH)

    sibling = dev(xlo, z, y, xhi, 1 - core)
    partner = dev(1 - xlo, z, y, xhi, core)
    up = dev(xlo, (z + 1) % NZ, y, xhi, core)
    down = dev(xlo, (z + NZ - 1) % NZ, y, xhi, core)

    barrier = pltpu.get_barrier_semaphore()

    def greet(to):
        pl.semaphore_signal(barrier, inc=1, device_id=to, device_id_type=MESH)

    def along_x(dx):
        x = (xhi * 2 + xlo + dx) % 4
        return dev(x % 2, z, y, x // 2, core)

    def along_y(dy):
        return dev(xlo, z, (y + dy) % 4, xhi, core)

    def along_z(dz):
        return dev(xlo, (z + dz + NZ) % NZ, y, xhi, core)

    near = [up, down, {"seq": (s + 1) % NS, "chan": c}, {"seq": (s + NS - 1) % NS, "chan": c}, sibling,
            along_x(1), along_x(3), along_y(1), along_y(3)]
    for to in near:
        greet(to)

    def tell(n, to):
        pl.semaphore_signal(know.at[n], inc=1, device_id=to, device_id_type=MESH)

    def heard(n):
        pl.semaphore_wait(know.at[n], 1)

    load_f = pltpu.make_async_copy(feat, fraw, ls.at[Q])
    load_f.start()
    own_w = [pltpu.make_async_copy(w.at[:, pl.ds(n * WIDE, WIDE)], wbuf.at[n, z], ls.at[n]) for n in range(2)]
    for o in own_w:
        o.start()
    small = [pltpu.make_async_copy(a, b, ls.at[Q + 1 + n]) for n, (a, b) in enumerate(
        ((taps_h, taps), (dec_h, dec), (res_h, res), (sin_h, sin), (stream_h, stream)))]
    for o in small:
        o.start()
    load_f.wait()
    for i in range(3):
        fpad[i, pl.ds(8, T), :] = fraw[i].astype(F32)
        tail[pl.ds(2 * i, 2), :] = fpad[i, pl.ds(8 + T - 2, 2), :]
    tail[pl.ds(6, 2), :] = jnp.zeros((2, Q * LANES), F32)
    for o in own_w + small:
        o.wait()

    pl.semaphore_wait(barrier, len(near))

    send_halo = remote(tail, halo, hs.at[0], hs.at[1], {"seq": (s + 1) % NS, "chan": c})
    send_halo.start()

    def chunk(block, q):
        return wbuf.at[q // 2, block, pl.ds(q % 2 * LANES, LANES)]

    def w_copy(way, j, q):
        block = (z + NZ - j) % NZ if way == 0 else (z + j) % NZ
        return remote(chunk(block, q), chunk(block, q), ws.at[way, j, q], wr.at[way, j, q], up if way == 0 else down)

    def w_arrived(way, j, q):
        block = (z + NZ - j - 1) % NZ if way == 0 else (z + j + 1) % NZ
        return remote(chunk(block, q), chunk(block, q), ws.at[way, j, q], wr.at[way, j, q], up if way == 0 else down)

    sent = []

    def w_send(way, j, q):
        copy = w_copy(way, j, q)
        copy.start()
        sent.append((way, j, q))

    for q in range(Q):
        w_send(0, 0, q)
        w_send(1, 0, q)

    tell(0, up)
    tell(1, down)
    tell(6, along_y(3))
    tell(7, along_x(3))

    forwards = [(j, q) for j in range(1, 8) for q in range(Q)]

    def until(t):
        while forwards and FIRST + EACH * (4 * (forwards[0][0] - 1) + forwards[0][1]) <= t:
            j, q = forwards.pop(0)
            for way in (0, 1):
                w_arrived(way, j - 1, q).wait_recv()
                if j < 7 or q % 2 == way:
                    w_send(way, j, q)

    send_halo.wait_recv()
    heard(0)
    heard(1)
    tell(2, along_z(2))
    tell(3, along_z(-2))
    first = s > 0
    for i in range(3):
        fpad[i, pl.ds(6, 2), :] = jnp.where(first, halo[pl.ds(2 * i, 2), :], 0.0)

    def conv(q, carry):
        cols = pl.ds(pl.multiple_of(q * LANES, LANES), LANES)

        def short(i):
            total = taps[i, 0:1, cols] * fpad[i, pl.ds(8, T), cols]
            total = total + taps[i, 1:2, cols] * fpad[i, pl.ds(7, T), cols]
            return total + taps[i, 2:3, cols] * fpad[i, pl.ds(6, T), cols]

        pbuf[q] = short(1) * short(2)
        qbuf[q] = short(0)
        return carry

    lax.fori_loop(0, Q, conv, 0)

    row = lax.broadcasted_iota(jnp.int32, (SUB, LANES), 0)

    def inner(q, carry):
        cols = pl.ds(pl.multiple_of(q * LANES, LANES), LANES)
        rates = [jnp.broadcast_to(dec[r:r + 1, cols], (SUB, LANES)) for r in range(POLES)]
        step = [jnp.exp(-v) for v in rates]
        gain = [jnp.broadcast_to(res[r:r + 1, cols], (SUB, LANES)) for r in range(POLES)]
        x = [jnp.zeros((SUB, LANES), F32) for _ in range(POLES)]
        for j in range(STEPS):
            p = pbuf[q, pl.ds(j, SUB, stride=STEPS), :]
            x = [step[r] * x[r] + p for r in range(POLES)]
            ybuf[q, j] = sum(gain[r] * x[r] for r in range(POLES))
        for r in range(POLES):
            total = step[r] * x[r]
            for d in (1, 2, 4):
                moved = jnp.where(row >= d, pltpu.roll(total, d, 0), 0.0)
                total = total + jnp.exp(rates[r] * (-1.0 * STEPS * d)) * moved
            xs[q, r] = jnp.where(row >= 1, pltpu.roll(total, 1, 0), 0.0)
            ends[q * 4 + r // 2, r % 2:r % 2 + 1, :] = total[SUB - 1:SUB, :]
        return carry

    lax.fori_loop(0, Q, inner, 0)

    for q in range(Q):
        for p in range(4):
            part = (slice(2 * p, 2 * p + 2), slice(q * LANES, (q + 1) * LANES))
            dec16[q * 4 + p] = dec[part]
            sin16[q * 4 + p] = sin[part]

    def end_copy(n):
        to = (z + n) % NZ
        return remote(ends.at[to], ends_in.at[z], es.at[n], er.at[z], along_z(n))

    def end_arrives(n):
        came = (z + n) % NZ
        return remote(ends.at[0], ends_in.at[came], es.at[n], er.at[came], up)

    def start_copy(n):
        to = (z + n) % NZ
        return remote(starts.at[to], starts_in.at[z], ts.at[n], tr.at[z], along_z(n))

    def start_arrives(n):
        came = (z + n) % NZ
        return remote(starts.at[0], starts_in.at[came], ts.at[n], tr.at[came], up)

    def each(lo, hi, do):
        def step(n, carry):
            do(n)
            return carry

        lax.fori_loop(lo, hi, step, 0)

    until(KNOW_AT[1])
    heard(2)
    heard(3)
    tell(4, along_z(4))
    tell(5, along_z(-4))
    each(1, 5, lambda n: end_copy(n).start())
    each(12, 16, lambda n: end_copy(n).start())
    ends_in[z] = ends[z]
    until(KNOW_AT[2])
    heard(4)
    heard(5)
    each(5, 12, lambda n: end_copy(n).start())
    until(ENDS_AT)
    each(1, 16, lambda n: end_arrives(n).wait_recv())
    rate = jnp.exp(dec16[z] * (-1.0 * T))
    give_total = remote(total_out, total_in, ps.at[0], ps.at[1], partner)

    @pl.when(xlo == 0)
    def _():
        seed[...] = sin16[z]

    @pl.when(xlo == 1)
    def _():
        give_total.wait_recv()
        seed[...] = total_in[...]

    state = seed[...]
    for n in range(NZ):
        starts[n] = state
        state = rate * state + ends_in[n]

    @pl.when(xlo == 0)
    def _():
        total_out[...] = state
        give_total.start()

    each(1, 16, lambda n: start_copy(n).start())
    starts_in[z] = starts[z]
    until(STARTS_AT)
    each(1, 16, lambda n: start_arrives(n).wait_recv())
    for q in range(Q):
        for p in range(4):
            sbuf[q, 2 * p:2 * p + 2, :] = starts_in[q * 4 + p]

    def gate(q, carry):
        cols = pl.ds(pl.multiple_of(q * LANES, LANES), LANES)
        rates = [jnp.broadcast_to(dec[r:r + 1, cols], (SUB, LANES)) for r in range(POLES)]
        step = [jnp.exp(-v) for v in rates]
        back = row.astype(F32) * (-1.0 * STEPS)
        x = []
        for r in range(POLES):
            start = xs[q, r] + jnp.exp(rates[r] * back) * sbuf[q, r:r + 1, :]
            x.append(res[r:r + 1, cols] * start)
        for j in range(STEPS):
            total = ybuf[q, j] + sum(x)
            x = [step[r] * x[r] for r in range(POLES)]
            rows = pl.ds(j, SUB, stride=STEPS)
            gf[q, rows, :] = total * qbuf[q, rows, :]
        gown[q // 2, :, pl.ds(pl.multiple_of((q % 2) * LANES, LANES), LANES)] = gf[q].astype(jnp.bfloat16)
        return carry

    lax.fori_loop(0, Q, gate, 0)

    def spot(yy):
        other = (yy // 2 + xlo) % 2
        k = ((yy % 2) * 4 + xhi * 2 + core) * (1 - other) + (yy % 2) * other
        return gall.at[xlo * (1 - other) + 2 * other, pl.ds(2 * k, 2)]

    def landing(yy):
        k = (yy % 2) * 4 + xhi * 2 + core
        return gall.at[xlo, pl.ds(2 * k, 2)], gr.at[xlo, k]

    def send_x(n, src):
        yy = (y + n) % 4
        dst, sem = landing(yy)
        same = yy // 2 == xlo

        @pl.when(same)
        def _():
            remote(src, dst, gs.at[n, 0], sem, along_x(2)).start()

        @pl.when(jnp.logical_not(same))
        def _():
            remote(src, dst, gs.at[n, 0], sem, along_x(1)).start()
            remote(src, dst, gs.at[n, 1], sem, along_x(3)).start()

    heard(6)
    heard(7)
    home = y // 2 == xlo

    @pl.when(home)
    def _():
        pltpu.make_async_copy(gown, spot(y), sr.at[y]).start()

    send_x(0, gown)
    y_sends = [remote(gown, spot(y), ys.at[n], sr.at[y], along_y(n)) for n in (1, 2, 3)]
    for copy in y_sends:
        copy.start()
    passed = []

    def to_sibling(slot, sem):
        copy = remote(slot, slot, fs.at[len(passed)], sem, sibling)
        copy.start()
        passed.append((slot, sem))

    for n in (1, 3, 2):
        until(Y_AT[n])
        yy = (y + n) % 4
        remote(spot(yy), spot(yy), ys.at[n], sr.at[yy], sibling).wait_recv()
        send_x(n, spot(yy))

    def arrived(xl, yy, xh, co):
        k = yy * 4 + xh * 2 + co
        return gall.at[xl, pl.ds(2 * k, 2)], gr.at[xl, k]

    @pl.when(home)
    def _():
        pltpu.make_async_copy(gown, spot(y), sr.at[y]).wait()

    for yy in range(2):
        to_sibling(*arrived(xlo, yy, xhi, core))
    for yy in range(2):
        for xl, xh in ((1 - xlo, xhi), (1 - xlo, 1 - xhi), (xlo, 1 - xhi)):
            until(X_AT[len(passed) - 2])
            slot, sem = arrived(xl, yy, xh, core)
            remote(slot, slot, fs.at[0], sem, sibling).wait_recv()
            to_sibling(slot, sem)
    until(SIBLING_AT)
    for xl in range(2):
        for yy in range(2):
            for xh in range(2):
                slot, sem = arrived(xl, yy, xh, 1 - core)
                remote(slot, slot, fs.at[0], sem, sibling).wait_recv()

    def add(n, block, fresh=False):
        lhs = gall[pl.ds(0, 2), block].reshape(2 * T, WIDE)
        part = jnp.dot(lhs, wbuf[n, block], preferred_element_type=F32)
        acc[n] = part if fresh else acc[n] + part

    clock = SIBLING_AT
    for n in range(2):
        add(n, z, fresh=True)
    for i in range(1, 8):
        for block in ((z + i) % NZ, (z + NZ - i) % NZ):
            clock += DOT
            until(clock)
            while forwards and forwards[0][0] <= i:
                until(FIRST + EACH * (4 * (forwards[0][0] - 1) + forwards[0][1]))
            for n in range(2):
                add(n, block)
    sums = []
    for n in range(2):
        for way in (0, 1):
            w_arrived(way, 7, 2 * n + way).wait_recv()
        add(n, (z + 8) % NZ)
        csrc[n] = acc[n, pl.ds(pl.multiple_of((1 - xlo) * T, T), T), :].astype(jnp.bfloat16)
        copy = remote(csrc.at[n], cbuf.at[n], cs.at[n], cr.at[n], partner)
        copy.start()
        sums.append(copy)
    for n, copy in enumerate(sums):
        copy.wait_recv()
        cols = pl.ds(n * WIDE, WIDE)
        mixed = acc[n, pl.ds(pl.multiple_of(xlo * T, T), T), :] + cbuf[n].astype(F32)
        out[:, cols] = (stream[:, cols].astype(F32) + mixed).astype(jnp.bfloat16)

    for copy in sums:
        copy.wait_send()
    for n, (slot, sem) in enumerate(passed):
        remote(slot, slot, fs.at[n], sem, sibling).wait_send()
    each(1, 16, lambda n: end_copy(n).wait_send())
    each(1, 16, lambda n: start_copy(n).wait_send())

    @pl.when(xlo == 0)
    def _():
        give_total.wait_send()

    send_halo.wait_send()
    for way, j, q in sent:
        w_copy(way, j, q).wait_send()
    for copy in y_sends:
        copy.wait_send()
    for n in range(4):
        dst, sem = landing((y + n) % 4)
        remote(gown, dst, gs.at[n, 0], sem, sibling).wait_send()

        @pl.when((y + n) % 4 // 2 != xlo)
        def _():
            remote(gown, dst, gs.at[n, 1], sem, sibling).wait_send()


def shards(stream_in, features, conv_taps, decay, residues, state_in, out_weight):
    vmem = pl.BlockSpec(memory_space=pltpu.VMEM)
    hbm = pl.BlockSpec(memory_space=pl.ANY)
    D = Q * LANES
    dma = pltpu.SemaphoreType.DMA
    return pl.pallas_call(
        kernel,
        out_shape=jax.ShapeDtypeStruct((T, D), jnp.bfloat16),
        in_specs=[hbm] * 7,
        out_specs=vmem,
        scratch_shapes=[
            pltpu.VMEM((3, 3, D), F32),
            pltpu.VMEM((POLES, D), F32),
            pltpu.VMEM((POLES, D), F32),
            pltpu.VMEM((POLES, D), F32),
            pltpu.VMEM((T, D), jnp.bfloat16),
            pltpu.VMEM((2, NZ, WIDE, WIDE), jnp.bfloat16),
            pltpu.VMEM((3, NZ, T, 2 * LANES), jnp.bfloat16),
            pltpu.VMEM((2, T, 2 * LANES), jnp.bfloat16),
            pltpu.VMEM((3, T, D), jnp.bfloat16),
            pltpu.VMEM((3, T + 8, D), F32),
            pltpu.VMEM((8, D), F32),
            pltpu.VMEM((8, D), F32),
            pltpu.VMEM((Q, T, LANES), F32),
            pltpu.VMEM((Q, T, LANES), F32),
            pltpu.VMEM((Q, STEPS, SUB, LANES), F32),
            pltpu.VMEM((Q, POLES, SUB, LANES), F32),
            pltpu.VMEM((Q, T, LANES), F32),
            *[pltpu.VMEM((NZ, 2, LANES), F32)] * 6,
            *[pltpu.VMEM((2, LANES), F32)] * 3,
            pltpu.VMEM((Q, POLES, LANES), F32),
            pltpu.VMEM((2, 2 * T, WIDE), F32),
            pltpu.VMEM((2, T, WIDE), jnp.bfloat16),
            pltpu.VMEM((2, T, WIDE), jnp.bfloat16),
            dma((2, 8, Q)), dma((2, 8, Q)),
            dma((4, 2)), dma((2, 8)), dma((4,)), dma((4,)), dma((8,)),
            dma((NZ,)), dma((NZ,)), dma((NZ,)), dma((NZ,)), dma((2,)),
            dma((2,)), dma((2,)), dma((2,)), dma((Q + 6,)),
            pltpu.SemaphoreType.REGULAR((8,)),
        ],
        compiler_params=pltpu.CompilerParams(
            collective_id=0, has_side_effects=True, vmem_limit_bytes=60 * 2**20),
    )(features, conv_taps, decay.T, residues.T, state_in.T, stream_in, out_weight)


def solution(mesh):
    return jax.shard_map(
        shards,
        mesh=mesh,
        in_specs=(
            P("seq", "chan"),
            P(None, "seq", "chan"),
            P(None, None, "chan"),
            P("chan", None),
            P("chan", None),
            P("chan", None),
            P("seq", "chan"),
        ),
        out_specs=P("seq", "chan"),
        check_vma=False,
    )
```

```python
import jax
import jax.numpy as jnp
from jax import lax
from jax.experimental import pallas as pl
from jax.experimental.pallas import tpu as pltpu
from jax.sharding import PartitionSpec as P

FIRST, EACH = 4.2, 1.42
KNOW_AT = (2.5, 6.0, 11.0)
ENDS_AT, TOTAL_AT, STARTS_AT = 17.5, 18.0, 26.0
Y_AT = (30.5, 31.0, 32.0, 32.5, 33.5, 34.5)
X_AT = (34.5, 34.5, 34.5, 35.5, 35.5, 35.5, 37.0, 37.5, 38.0, 39.0, 40.0, 40.5)
SIBLING_AT = 41.0
DOT = 0.25

MESH = pl.DeviceIdType.MESH
F32 = jnp.float32
LANES = 128
WIDE = 256
Q = 4
POLES = 8
T = 128
SUB = 8
STEPS = T // SUB
NZ = 16
NS = 32


def place():
    s = lax.axis_index("seq")
    c = lax.axis_index("chan")
    return s, c, s // NZ, s % NZ, c // 4, (c // 2) % 2, c % 2


def kernel(feat, taps_h, dec_h, res_h, sin_h, stream_h, w, out,
           taps, dec, res, sin, stream, wbuf, gall, gown, fraw, fpad, tail, halo, pbuf, qbuf, ybuf, xs, gf, ends, ends_in, starts, starts_in, dec16, sin16, seed, total_out, total_in, sbuf, acc, csrc, cbuf,
           ws, wr, gs, gr, ys, sr, fs, es, er, ts, tr, ps, hs, cs, cr, ls, know):
    s, c, xlo, z, y, xhi, core = place()

    def dev(xl, zz, yy, xh, co):
        return {"seq": xl * NZ + zz, "chan": yy * 4 + xh * 2 + co}

    def remote(src, dst, ssem, rsem, to):
        return pltpu.make_async_remote_copy(
            src_ref=src, dst_ref=dst, send_sem=ssem, recv_sem=rsem, device_id=to, device_id_type=MESH)

    sibling = dev(xlo, z, y, xhi, 1 - core)
    partner = dev(1 - xlo, z, y, xhi, core)
    up = dev(xlo, (z + 1) % NZ, y, xhi, core)
    down = dev(xlo, (z + NZ - 1) % NZ, y, xhi, core)

    barrier = pltpu.get_barrier_semaphore()

    def greet(to):
        pl.semaphore_signal(barrier, inc=1, device_id=to, device_id_type=MESH)

    def along_x(dx):
        x = (xhi * 2 + xlo + dx) % 4
        return dev(x % 2, z, y, x // 2, core)

    def along_y(dy):
        return dev(xlo, z, (y + dy) % 4, xhi, core)

    def along_z(dz):
        return dev(xlo, (z + dz + NZ) % NZ, y, xhi, core)

    near = [up, down, {"seq": (s + 1) % NS, "chan": c}, {"seq": (s + NS - 1) % NS, "chan": c}, sibling,
            along_x(1), along_x(3), along_y(1), along_y(3)]
    for to in near:
        greet(to)

    def tell(n, to):
        pl.semaphore_signal(know.at[n], inc=1, device_id=to, device_id_type=MESH)

    def heard(n):
        pl.semaphore_wait(know.at[n], 1)

    load_f = pltpu.make_async_copy(feat, fraw, ls.at[Q])
    load_f.start()
    own_w = [pltpu.make_async_copy(w.at[:, pl.ds(n * WIDE, WIDE)], wbuf.at[n, z], ls.at[n]) for n in range(2)]
    for o in own_w:
        o.start()
    small = [pltpu.make_async_copy(a, b, ls.at[Q + 1 + n]) for n, (a, b) in enumerate(
        ((taps_h, taps), (dec_h, dec), (res_h, res), (sin_h, sin), (stream_h, stream)))]
    for o in small:
        o.start()
    load_f.wait()
    for i in range(3):
        fpad[i, pl.ds(8, T), :] = fraw[i].astype(F32)
        tail[pl.ds(2 * i, 2), :] = fpad[i, pl.ds(8 + T - 2, 2), :]
    tail[pl.ds(6, 2), :] = jnp.zeros((2, Q * LANES), F32)
    for o in own_w + small:
        o.wait()

    pl.semaphore_wait(barrier, len(near))

    send_halo = remote(tail, halo, hs.at[0], hs.at[1], {"seq": (s + 1) % NS, "chan": c})
    send_halo.start()

    def chunk(block, q):
        return wbuf.at[q // 2, block, pl.ds(q % 2 * LANES, LANES)]

    def w_copy(way, j, q):
        block = (z + NZ - j) % NZ if way == 0 else (z + j) % NZ
        return remote(chunk(block, q), chunk(block, q), ws.at[way, j, q], wr.at[way, j, q], up if way == 0 else down)

    def w_arrived(way, j, q):
        block = (z + NZ - j - 1) % NZ if way == 0 else (z + j + 1) % NZ
        return remote(chunk(block, q), chunk(block, q), ws.at[way, j, q], wr.at[way, j, q], up if way == 0 else down)

    sent = []

    def w_send(way, j, q):
        copy = w_copy(way, j, q)
        copy.start()
        sent.append((way, j, q))

    for q in range(Q):
        w_send(0, 0, q)
        w_send(1, 0, q)

    tell(0, up)
    tell(1, down)
    tell(6, along_y(3))
    tell(7, along_x(3))

    forwards = [(j, q) for j in range(1, 8) for q in range(Q)]

    def until(t):
        while forwards and FIRST + EACH * (4 * (forwards[0][0] - 1) + forwards[0][1]) <= t:
            j, q = forwards.pop(0)
            for way in (0, 1):
                w_arrived(way, j - 1, q).wait_recv()
                if j < 7 or q % 2 == way:
                    w_send(way, j, q)

    send_halo.wait_recv()
    heard(0)
    heard(1)
    tell(2, along_z(2))
    tell(3, along_z(-2))
    first = s > 0
    for i in range(3):
        fpad[i, pl.ds(6, 2), :] = jnp.where(first, halo[pl.ds(2 * i, 2), :], 0.0)

    def conv(q, carry):
        cols = pl.ds(pl.multiple_of(q * LANES, LANES), LANES)

        def short(i):
            total = taps[i, 0:1, cols] * fpad[i, pl.ds(8, T), cols]
            total = total + taps[i, 1:2, cols] * fpad[i, pl.ds(7, T), cols]
            return total + taps[i, 2:3, cols] * fpad[i, pl.ds(6, T), cols]

        pbuf[q] = short(1) * short(2)
        qbuf[q] = short(0)
        return carry

    lax.fori_loop(0, Q, conv, 0)

    row = lax.broadcasted_iota(jnp.int32, (SUB, LANES), 0)

    def inner(q, carry):
        cols = pl.ds(pl.multiple_of(q * LANES, LANES), LANES)
        rates = [jnp.broadcast_to(dec[r:r + 1, cols], (SUB, LANES)) for r in range(POLES)]
        step = [jnp.exp(-v) for v in rates]
        gain = [jnp.broadcast_to(res[r:r + 1, cols], (SUB, LANES)) for r in range(POLES)]
        x = [jnp.zeros((SUB, LANES), F32) for _ in range(POLES)]
        for j in range(STEPS):
            p = pbuf[q, pl.ds(j, SUB, stride=STEPS), :]
            x = [step[r] * x[r] + p for r in range(POLES)]
            ybuf[q, j] = sum(gain[r] * x[r] for r in range(POLES))
        for r in range(POLES):
            total = step[r] * x[r]
            for d in (1, 2, 4):
                moved = jnp.where(row >= d, pltpu.roll(total, d, 0), 0.0)
                total = total + jnp.exp(rates[r] * (-1.0 * STEPS * d)) * moved
            xs[q, r] = jnp.where(row >= 1, pltpu.roll(total, 1, 0), 0.0)
            ends[q * 4 + r // 2, r % 2:r % 2 + 1, :] = total[SUB - 1:SUB, :]
        return carry

    lax.fori_loop(0, Q, inner, 0)

    for q in range(Q):
        for p in range(4):
            part = (slice(2 * p, 2 * p + 2), slice(q * LANES, (q + 1) * LANES))
            dec16[q * 4 + p] = dec[part]
            sin16[q * 4 + p] = sin[part]

    def end_copy(n):
        to = (z + n) % NZ
        return remote(ends.at[to], ends_in.at[z], es.at[n], er.at[z], along_z(n))

    def end_arrives(n):
        came = (z + n) % NZ
        return remote(ends.at[0], ends_in.at[came], es.at[n], er.at[came], up)

    def start_copy(n):
        to = (z + n) % NZ
        return remote(starts.at[to], starts_in.at[z], ts.at[n], tr.at[z], along_z(n))

    def start_arrives(n):
        came = (z + n) % NZ
        return remote(starts.at[0], starts_in.at[came], ts.at[n], tr.at[came], up)

    def each(lo, hi, do):
        def step(n, carry):
            do(n)
            return carry

        lax.fori_loop(lo, hi, step, 0)

    until(KNOW_AT[1])
    heard(2)
    heard(3)
    tell(4, along_z(4))
    tell(5, along_z(-4))
    each(1, 5, lambda n: end_copy(n).start())
    each(12, 16, lambda n: end_copy(n).start())
    ends_in[z] = ends[z]
    until(KNOW_AT[2])
    heard(4)
    heard(5)
    each(5, 12, lambda n: end_copy(n).start())
    until(ENDS_AT)
    each(1, 16, lambda n: end_arrives(n).wait_recv())
    rate = jnp.exp(dec16[z] * (-1.0 * T))
    give_total = remote(total_out, total_in, ps.at[0], ps.at[1], partner)

    @pl.when(xlo == 0)
    def _():
        seed[...] = sin16[z]

    @pl.when(xlo == 1)
    def _():
        give_total.wait_recv()
        seed[...] = total_in[...]

    state = seed[...]
    for n in range(NZ):
        starts[n] = state
        state = rate * state + ends_in[n]

    @pl.when(xlo == 0)
    def _():
        total_out[...] = state
        give_total.start()

    each(1, 16, lambda n: start_copy(n).start())
    starts_in[z] = starts[z]
    until(STARTS_AT)
    each(1, 16, lambda n: start_arrives(n).wait_recv())
    for q in range(Q):
        for p in range(4):
            sbuf[q, 2 * p:2 * p + 2, :] = starts_in[q * 4 + p]

    def gate(q, carry):
        cols = pl.ds(pl.multiple_of(q * LANES, LANES), LANES)
        rates = [jnp.broadcast_to(dec[r:r + 1, cols], (SUB, LANES)) for r in range(POLES)]
        step = [jnp.exp(-v) for v in rates]
        back = row.astype(F32) * (-1.0 * STEPS)
        x = []
        for r in range(POLES):
            start = xs[q, r] + jnp.exp(rates[r] * back) * sbuf[q, r:r + 1, :]
            x.append(res[r:r + 1, cols] * start)
        for j in range(STEPS):
            total = ybuf[q, j] + sum(x)
            x = [step[r] * x[r] for r in range(POLES)]
            rows = pl.ds(j, SUB, stride=STEPS)
            gf[q, rows, :] = total * qbuf[q, rows, :]
        gown[q // 2, :, pl.ds(pl.multiple_of((q % 2) * LANES, LANES), LANES)] = gf[q].astype(jnp.bfloat16)
        return carry

    def spot(yy, h):
        other = (yy // 2 + xlo) % 2
        k = ((yy % 2) * 4 + xhi * 2 + core) * (1 - other) + (yy % 2) * other
        return gall.at[xlo * (1 - other) + 2 * other, 2 * k + h]

    def landing(yy, h):
        k = (yy % 2) * 4 + xhi * 2 + core
        return gall.at[xlo, 2 * k + h], gr.at[xlo, k, h]

    def send_x(n, h, src):
        yy = (y + n) % 4
        dst, sem = landing(yy, h)
        same = yy // 2 == xlo

        @pl.when(same)
        def _():
            remote(src, dst, gs.at[n, 0, h], sem, along_x(2)).start()

        @pl.when(jnp.logical_not(same))
        def _():
            remote(src, dst, gs.at[n, 0, h], sem, along_x(1)).start()
            remote(src, dst, gs.at[n, 1, h], sem, along_x(3)).start()

    heard(6)
    heard(7)
    home = y // 2 == xlo
    y_sends = []
    for h in range(2):
        lax.fori_loop(2 * h, 2 * h + 2, gate, 0)

        @pl.when(home)
        def _():
            pltpu.make_async_copy(gown.at[h], spot(y, h), sr.at[y, h]).start()

        send_x(0, h, gown.at[h])
        for n in (1, 3, 2):
            copy = remote(gown.at[h], spot(y, h), ys.at[n, h], sr.at[y, h], along_y(n))
            copy.start()
            y_sends.append(copy)
    passed = []

    def to_sibling(slot, sem):
        copy = remote(slot, slot, fs.at[len(passed)], sem, sibling)
        copy.start()
        passed.append((slot, sem))

    for i, (n, h) in enumerate(((1, 0), (3, 0), (1, 1), (3, 1), (2, 0), (2, 1))):
        until(Y_AT[i])
        yy = (y + n) % 4
        remote(spot(yy, h), spot(yy, h), ys.at[n, h], sr.at[yy, h], sibling).wait_recv()
        send_x(n, h, spot(yy, h))

    def arrived(xl, yy, xh, co, h):
        k = yy * 4 + xh * 2 + co
        return gall.at[xl, 2 * k + h], gr.at[xl, k, h]

    @pl.when(home)
    def _():
        for h in range(2):
            pltpu.make_async_copy(gown.at[h], spot(y, h), sr.at[y, h]).wait()

    for yy in range(2):
        for h in range(2):
            to_sibling(*arrived(xlo, yy, xhi, core, h))
    nearer = (y + y // 2 + xlo) % 2
    for i in range(2):
        yy = (nearer + i) % 2
        for h in range(2):
            for xl, xh in ((1 - xlo, xhi), (1 - xlo, 1 - xhi), (xlo, 1 - xhi)):
                until(X_AT[len(passed) - 4])
                slot, sem = arrived(xl, yy, xh, core, h)
                remote(slot, slot, fs.at[0], sem, sibling).wait_recv()
                to_sibling(slot, sem)
    until(SIBLING_AT)
    for xl in range(2):
        for yy in range(2):
            for xh in range(2):
                for h in range(2):
                    slot, sem = arrived(xl, yy, xh, 1 - core, h)
                    remote(slot, slot, fs.at[0], sem, sibling).wait_recv()

    def add(n, block, fresh=False):
        lhs = gall[pl.ds(0, 2), block].reshape(2 * T, WIDE)
        part = jnp.dot(lhs, wbuf[n, block], preferred_element_type=F32)
        acc[n] = part if fresh else acc[n] + part

    clock = SIBLING_AT
    for n in range(2):
        add(n, z, fresh=True)
    for i in range(1, 8):
        for block in ((z + i) % NZ, (z + NZ - i) % NZ):
            clock += DOT
            until(clock)
            while forwards and forwards[0][0] <= i:
                until(FIRST + EACH * (4 * (forwards[0][0] - 1) + forwards[0][1]))
            for n in range(2):
                add(n, block)
    sums = []
    for n in range(2):
        for way in (0, 1):
            w_arrived(way, 7, 2 * n + way).wait_recv()
        add(n, (z + 8) % NZ)
        csrc[n] = acc[n, pl.ds(pl.multiple_of((1 - xlo) * T, T), T), :].astype(jnp.bfloat16)
        copy = remote(csrc.at[n], cbuf.at[n], cs.at[n], cr.at[n], partner)
        copy.start()
        sums.append(copy)
    for n, copy in enumerate(sums):
        copy.wait_recv()
        cols = pl.ds(n * WIDE, WIDE)
        mixed = acc[n, pl.ds(pl.multiple_of(xlo * T, T), T), :] + cbuf[n].astype(F32)
        out[:, cols] = (stream[:, cols].astype(F32) + mixed).astype(jnp.bfloat16)

    for copy in sums:
        copy.wait_send()
    for n, (slot, sem) in enumerate(passed):
        remote(slot, slot, fs.at[n], sem, sibling).wait_send()
    each(1, 16, lambda n: end_copy(n).wait_send())
    each(1, 16, lambda n: start_copy(n).wait_send())

    @pl.when(xlo == 0)
    def _():
        give_total.wait_send()

    send_halo.wait_send()
    for way, j, q in sent:
        w_copy(way, j, q).wait_send()
    for copy in y_sends:
        copy.wait_send()
    for n in range(4):
        for h in range(2):
            dst, sem = landing((y + n) % 4, h)
            remote(gown.at[h], dst, gs.at[n, 0, h], sem, sibling).wait_send()

            @pl.when((y + n) % 4 // 2 != xlo)
            def _():
                remote(gown.at[h], dst, gs.at[n, 1, h], sem, sibling).wait_send()


def shards(stream_in, features, conv_taps, decay, residues, state_in, out_weight):
    vmem = pl.BlockSpec(memory_space=pltpu.VMEM)
    hbm = pl.BlockSpec(memory_space=pl.ANY)
    D = Q * LANES
    dma = pltpu.SemaphoreType.DMA
    return pl.pallas_call(
        kernel,
        out_shape=jax.ShapeDtypeStruct((T, D), jnp.bfloat16),
        in_specs=[hbm] * 7,
        out_specs=vmem,
        scratch_shapes=[
            pltpu.VMEM((3, 3, D), F32),
            pltpu.VMEM((POLES, D), F32),
            pltpu.VMEM((POLES, D), F32),
            pltpu.VMEM((POLES, D), F32),
            pltpu.VMEM((T, D), jnp.bfloat16),
            pltpu.VMEM((2, NZ, WIDE, WIDE), jnp.bfloat16),
            pltpu.VMEM((3, NZ, T, 2 * LANES), jnp.bfloat16),
            pltpu.VMEM((2, T, 2 * LANES), jnp.bfloat16),
            pltpu.VMEM((3, T, D), jnp.bfloat16),
            pltpu.VMEM((3, T + 8, D), F32),
            pltpu.VMEM((8, D), F32),
            pltpu.VMEM((8, D), F32),
            pltpu.VMEM((Q, T, LANES), F32),
            pltpu.VMEM((Q, T, LANES), F32),
            pltpu.VMEM((Q, STEPS, SUB, LANES), F32),
            pltpu.VMEM((Q, POLES, SUB, LANES), F32),
            pltpu.VMEM((Q, T, LANES), F32),
            *[pltpu.VMEM((NZ, 2, LANES), F32)] * 6,
            *[pltpu.VMEM((2, LANES), F32)] * 3,
            pltpu.VMEM((Q, POLES, LANES), F32),
            pltpu.VMEM((2, 2 * T, WIDE), F32),
            pltpu.VMEM((2, T, WIDE), jnp.bfloat16),
            pltpu.VMEM((2, T, WIDE), jnp.bfloat16),
            dma((2, 8, Q)), dma((2, 8, Q)),
            dma((4, 2, 2)), dma((2, 8, 2)), dma((4, 2)), dma((4, 2)), dma((16,)),
            dma((NZ,)), dma((NZ,)), dma((NZ,)), dma((NZ,)), dma((2,)),
            dma((2,)), dma((2,)), dma((2,)), dma((Q + 6,)),
            pltpu.SemaphoreType.REGULAR((8,)),
        ],
        compiler_params=pltpu.CompilerParams(
            collective_id=0, has_side_effects=True, vmem_limit_bytes=60 * 2**20),
    )(features, conv_taps, decay.T, residues.T, state_in.T, stream_in, out_weight)


def solution(mesh):
    return jax.shard_map(
        shards,
        mesh=mesh,
        in_specs=(
            P("seq", "chan"),
            P(None, "seq", "chan"),
            P(None, None, "chan"),
            P("chan", None),
            P("chan", None),
            P("chan", None),
            P("seq", "chan"),
        ),
        out_specs=P("seq", "chan"),
        check_vma=False,
    )
```

```python
import jax
import jax.numpy as jnp
from jax import lax
from jax.experimental import pallas as pl
from jax.experimental.pallas import tpu as pltpu
from jax.sharding import PartitionSpec as P

FIRST, EACH = 4.2, 1.42
KNOW_AT = (2.5, 6.0, 9.5)
ENDS_AT, STARTS_AT = 17.5, 26.0
Y_AT = (30.5, 31.0, 32.0, 32.5, 33.5, 34.5)
X_AT = (34.5, 34.5, 34.5, 35.5, 35.5, 35.5, 37.0, 37.5, 38.0, 39.0, 40.0, 40.5)
SIBLING_AT = 44.0
DOT = 0.25

MESH = pl.DeviceIdType.MESH
F32 = jnp.float32
LANES = 128
WIDE = 256
Q = 4
POLES = 8
T = 128
SUB = 8
STEPS = T // SUB
NZ = 16
NS = 32


def place():
    s = lax.axis_index("seq")
    c = lax.axis_index("chan")
    return s, c, s // NZ, s % NZ, c // 4, (c // 2) % 2, c % 2


def kernel(feat, taps_h, dec_h, res_h, sin_h, stream_h, w, out,
           taps, dec, res, sin, stream, wbuf, gall, gown, fraw, fpad, tail, halo, pbuf, qbuf, ybuf, xs, gf, ends, ends_in, starts, starts_in, dec16, sin16, seed, total_out, total_in, sbuf, acc, csrc, cbuf,
           ws, wr, gs, gr, ys, sr, fs, es, er, ts, tr, ps, hs, cs, cr, ls, know):
    s, c, xlo, z, y, xhi, core = place()

    def dev(xl, zz, yy, xh, co):
        return {"seq": xl * NZ + zz, "chan": yy * 4 + xh * 2 + co}

    def remote(src, dst, ssem, rsem, to):
        return pltpu.make_async_remote_copy(
            src_ref=src, dst_ref=dst, send_sem=ssem, recv_sem=rsem, device_id=to, device_id_type=MESH)

    sibling = dev(xlo, z, y, xhi, 1 - core)
    partner = dev(1 - xlo, z, y, xhi, core)
    up = dev(xlo, (z + 1) % NZ, y, xhi, core)
    down = dev(xlo, (z + NZ - 1) % NZ, y, xhi, core)

    barrier = pltpu.get_barrier_semaphore()

    def greet(to):
        pl.semaphore_signal(barrier, inc=1, device_id=to, device_id_type=MESH)

    def along_x(dx):
        x = (xhi * 2 + xlo + dx) % 4
        return dev(x % 2, z, y, x // 2, core)

    def along_y(dy):
        return dev(xlo, z, (y + dy) % 4, xhi, core)

    def along_z(dz):
        return dev(xlo, (z + dz + NZ) % NZ, y, xhi, core)

    near = [up, down, {"seq": (s + 1) % NS, "chan": c}, {"seq": (s + NS - 1) % NS, "chan": c}, sibling,
            along_x(1), along_x(3), along_y(1), along_y(3)]
    for to in near:
        greet(to)

    def tell(n, to):
        pl.semaphore_signal(know.at[n], inc=1, device_id=to, device_id_type=MESH)

    def heard(n):
        pl.semaphore_wait(know.at[n], 1)

    load_f = pltpu.make_async_copy(feat, fraw, ls.at[Q])
    load_f.start()
    own_w = [pltpu.make_async_copy(w.at[:, pl.ds(n * WIDE, WIDE)], wbuf.at[n, z], ls.at[n]) for n in range(2)]
    for o in own_w:
        o.start()
    small = [pltpu.make_async_copy(a, b, ls.at[Q + 1 + n]) for n, (a, b) in enumerate(
        ((taps_h, taps), (dec_h, dec), (res_h, res), (sin_h, sin), (stream_h, stream)))]
    for o in small:
        o.start()

    load_f.wait()
    for i in range(3):
        fpad[i, pl.ds(8, T), :] = fraw[i].astype(F32)
        tail[pl.ds(2 * i, 2), :] = fpad[i, pl.ds(8 + T - 2, 2), :]
    tail[pl.ds(6, 2), :] = jnp.zeros((2, Q * LANES), F32)
    for o in own_w:
        o.wait()
    pl.semaphore_wait(barrier, len(near))
    send_halo = remote(tail, halo, hs.at[0], hs.at[1], {"seq": (s + 1) % NS, "chan": c})
    send_halo.start()
    tell(0, up)
    tell(1, down)
    tell(6, along_y(3))
    tell(7, along_x(3))

    def chunk(block, q):
        return wbuf.at[q // 2, block, pl.ds(q % 2 * LANES, LANES)]

    def w_copy(way, j, q):
        block = (z + NZ - j) % NZ if way == 0 else (z + j) % NZ
        return remote(chunk(block, q), chunk(block, q), ws.at[way, j, q], wr.at[way, j, q], up if way == 0 else down)

    def w_arrived(way, j, q):
        block = (z + NZ - j - 1) % NZ if way == 0 else (z + j + 1) % NZ
        return remote(chunk(block, q), chunk(block, q), ws.at[way, j, q], wr.at[way, j, q], up if way == 0 else down)

    sent = []

    def w_send(way, j, q):
        copy = w_copy(way, j, q)
        copy.start()
        sent.append((way, j, q))

    for q in range(Q):
        w_send(0, 0, q)
        w_send(1, 0, q)


    forwards = [(j, q) for j in range(1, 8) for q in range(Q)]

    def until(t):
        while forwards and FIRST + EACH * (4 * (forwards[0][0] - 1) + forwards[0][1]) <= t:
            j, q = forwards.pop(0)
            for way in (0, 1):
                w_arrived(way, j - 1, q).wait_recv()
                if j < 7 or q % 2 == way:
                    w_send(way, j, q)

    for o in small:
        o.wait()

    send_halo.wait_recv()
    heard(0)
    heard(1)
    tell(2, along_z(2))
    tell(3, along_z(-2))
    first = s > 0
    for i in range(3):
        fpad[i, pl.ds(6, 2), :] = jnp.where(first, halo[pl.ds(2 * i, 2), :], 0.0)

    def conv(q, carry):
        cols = pl.ds(pl.multiple_of(q * LANES, LANES), LANES)

        def short(i):
            total = taps[i, 0:1, cols] * fpad[i, pl.ds(8, T), cols]
            total = total + taps[i, 1:2, cols] * fpad[i, pl.ds(7, T), cols]
            return total + taps[i, 2:3, cols] * fpad[i, pl.ds(6, T), cols]

        pbuf[q] = short(1) * short(2)
        qbuf[q] = short(0)
        return carry

    lax.fori_loop(0, Q, conv, 0)

    row = lax.broadcasted_iota(jnp.int32, (SUB, LANES), 0)

    def inner(q, carry):
        cols = pl.ds(pl.multiple_of(q * LANES, LANES), LANES)
        rates = [jnp.broadcast_to(dec[r:r + 1, cols], (SUB, LANES)) for r in range(POLES)]
        step = [jnp.exp(-v) for v in rates]
        gain = [jnp.broadcast_to(res[r:r + 1, cols], (SUB, LANES)) for r in range(POLES)]
        x = [jnp.zeros((SUB, LANES), F32) for _ in range(POLES)]
        for j in range(STEPS):
            p = pbuf[q, pl.ds(j, SUB, stride=STEPS), :]
            x = [step[r] * x[r] + p for r in range(POLES)]
            ybuf[q, j] = sum(gain[r] * x[r] for r in range(POLES))
        for r in range(POLES):
            total = step[r] * x[r]
            for d in (1, 2, 4):
                moved = jnp.where(row >= d, pltpu.roll(total, d, 0), 0.0)
                total = total + jnp.exp(rates[r] * (-1.0 * STEPS * d)) * moved
            xs[q, r] = jnp.where(row >= 1, pltpu.roll(total, 1, 0), 0.0)
            ends[q * 4 + r // 2, r % 2:r % 2 + 1, :] = total[SUB - 1:SUB, :]
        return carry

    lax.fori_loop(0, Q, inner, 0)

    for q in range(Q):
        for p in range(4):
            part = (slice(2 * p, 2 * p + 2), slice(q * LANES, (q + 1) * LANES))
            dec16[q * 4 + p] = dec[part]
            sin16[q * 4 + p] = sin[part]

    def end_copy(n):
        to = (z + n) % NZ
        return remote(ends.at[to], ends_in.at[z], es.at[n], er.at[z], along_z(n))

    def end_arrives(n):
        came = (z + n) % NZ
        return remote(ends.at[0], ends_in.at[came], es.at[n], er.at[came], up)

    def start_copy(n):
        to = (z + n) % NZ
        return remote(starts.at[to], starts_in.at[z], ts.at[n], tr.at[z], along_z(n))

    def start_arrives(n):
        came = (z + n) % NZ
        return remote(starts.at[0], starts_in.at[came], ts.at[n], tr.at[came], up)

    def each(lo, hi, do):
        def step(n, carry):
            do(n)
            return carry

        lax.fori_loop(lo, hi, step, 0)

    heard(2)
    heard(3)
    tell(4, along_z(4))
    tell(5, along_z(-4))
    each(1, 5, lambda n: end_copy(n).start())
    each(12, 16, lambda n: end_copy(n).start())
    until(KNOW_AT[1])
    ends_in[z] = ends[z]
    until(KNOW_AT[2])
    heard(4)
    heard(5)
    each(5, 12, lambda n: end_copy(n).start())
    until(ENDS_AT)
    each(1, 16, lambda n: end_arrives(n).wait_recv())
    rate = jnp.exp(dec16[z] * (-1.0 * T))
    give_total = remote(total_out, total_in, ps.at[0], ps.at[1], partner)

    @pl.when(xlo == 0)
    def _():
        seed[...] = sin16[z]

    @pl.when(xlo == 1)
    def _():
        give_total.wait_recv()
        seed[...] = total_in[...]

    state = seed[...]
    for n in range(NZ):
        starts[n] = state
        state = rate * state + ends_in[n]

    @pl.when(xlo == 0)
    def _():
        total_out[...] = state
        give_total.start()

    each(1, 16, lambda n: start_copy(n).start())
    starts_in[z] = starts[z]
    until(STARTS_AT)
    each(1, 16, lambda n: start_arrives(n).wait_recv())
    for q in range(Q):
        for p in range(4):
            sbuf[q, 2 * p:2 * p + 2, :] = starts_in[q * 4 + p]

    def gate(q, carry):
        cols = pl.ds(pl.multiple_of(q * LANES, LANES), LANES)
        rates = [jnp.broadcast_to(dec[r:r + 1, cols], (SUB, LANES)) for r in range(POLES)]
        step = [jnp.exp(-v) for v in rates]
        back = row.astype(F32) * (-1.0 * STEPS)
        x = []
        for r in range(POLES):
            start = xs[q, r] + jnp.exp(rates[r] * back) * sbuf[q, r:r + 1, :]
            x.append(res[r:r + 1, cols] * start)
        for j in range(STEPS):
            total = ybuf[q, j] + sum(x)
            x = [step[r] * x[r] for r in range(POLES)]
            rows = pl.ds(j, SUB, stride=STEPS)
            gf[q, rows, :] = total * qbuf[q, rows, :]
        gown[q // 2, :, pl.ds(pl.multiple_of((q % 2) * LANES, LANES), LANES)] = gf[q].astype(jnp.bfloat16)
        return carry

    def spot(yy, h):
        other = (yy // 2 + xlo) % 2
        k = ((yy % 2) * 4 + xhi * 2 + core) * (1 - other) + (yy % 2) * other
        return gall.at[xlo * (1 - other) + 2 * other, 2 * k + h]

    def landing(yy, h):
        k = (yy % 2) * 4 + xhi * 2 + core
        return gall.at[xlo, 2 * k + h], gr.at[xlo, k, h]

    def send_x(n, h, src):
        yy = (y + n) % 4
        dst, sem = landing(yy, h)
        same = yy // 2 == xlo

        @pl.when(same)
        def _():
            remote(src, dst, gs.at[n, 0, h], sem, along_x(2)).start()

        @pl.when(jnp.logical_not(same))
        def _():
            remote(src, dst, gs.at[n, 0, h], sem, along_x(1)).start()
            remote(src, dst, gs.at[n, 1, h], sem, along_x(3)).start()

    heard(6)
    heard(7)
    home = y // 2 == xlo
    y_sends = []
    for h in range(2):
        lax.fori_loop(2 * h, 2 * h + 2, gate, 0)

        @pl.when(home)
        def _():
            pltpu.make_async_copy(gown.at[h], spot(y, h), sr.at[y, h]).start()

        for n in (1, 3, 2):
            copy = remote(gown.at[h], spot(y, h), ys.at[n, h], sr.at[y, h], along_y(n))
            copy.start()
            y_sends.append(copy)
        send_x(0, h, gown.at[h])
    passed = []

    def to_sibling(slot, sem):
        copy = remote(slot, slot, fs.at[len(passed)], sem, sibling)
        copy.start()
        passed.append((slot, sem))

    for i, (n, h) in enumerate(((1, 0), (3, 0), (1, 1), (3, 1), (2, 0), (2, 1))):
        until(Y_AT[i])
        yy = (y + n) % 4
        remote(spot(yy, h), spot(yy, h), ys.at[n, h], sr.at[yy, h], sibling).wait_recv()
        send_x(n, h, spot(yy, h))

    def arrived(xl, yy, xh, co, h):
        k = yy * 4 + xh * 2 + co
        return gall.at[xl, 2 * k + h], gr.at[xl, k, h]

    @pl.when(home)
    def _():
        for h in range(2):
            pltpu.make_async_copy(gown.at[h], spot(y, h), sr.at[y, h]).wait()

    for yy in range(2):
        for h in range(2):
            to_sibling(*arrived(xlo, yy, xhi, core, h))
    nearer = (y + y // 2 + xlo) % 2
    for i in range(2):
        yy = (nearer + i) % 2
        for h in range(2):
            for xl, xh in ((1 - xlo, xhi), (1 - xlo, 1 - xhi), (xlo, 1 - xhi)):
                until(X_AT[len(passed) - 4])
                slot, sem = arrived(xl, yy, xh, core, h)
                remote(slot, slot, fs.at[0], sem, sibling).wait_recv()
                to_sibling(slot, sem)
    until(SIBLING_AT)
    for xl in range(2):
        for yy in range(2):
            for xh in range(2):
                for h in range(2):
                    slot, sem = arrived(xl, yy, xh, 1 - core, h)
                    remote(slot, slot, fs.at[0], sem, sibling).wait_recv()

    def add(n, block, fresh=False):
        lhs = gall[pl.ds(0, 2), block].reshape(2 * T, WIDE)
        part = jnp.dot(lhs, wbuf[n, block], preferred_element_type=F32)
        acc[n] = part if fresh else acc[n] + part

    clock = SIBLING_AT
    for n in range(2):
        add(n, z, fresh=True)
    for i in range(1, 8):
        for block in ((z + i) % NZ, (z + NZ - i) % NZ):
            clock += DOT
            until(clock)
            while forwards and forwards[0][0] <= i:
                until(FIRST + EACH * (4 * (forwards[0][0] - 1) + forwards[0][1]))
            for n in range(2):
                add(n, block)
    for n, (slot, sem) in enumerate(passed):
        remote(slot, slot, fs.at[n], sem, sibling).wait_send()
    each(1, 16, lambda n: end_copy(n).wait_send())
    each(1, 16, lambda n: start_copy(n).wait_send())

    @pl.when(xlo == 0)
    def _():
        give_total.wait_send()

    send_halo.wait_send()
    for way, j, q in sent:
        if j < 7:
            w_copy(way, j, q).wait_send()
    for copy in y_sends:
        copy.wait_send()
    for n in range(4):
        for h in range(2):
            dst, sem = landing((y + n) % 4, h)
            remote(gown.at[h], dst, gs.at[n, 0, h], sem, sibling).wait_send()

            @pl.when((y + n) % 4 // 2 != xlo)
            def _():
                remote(gown.at[h], dst, gs.at[n, 1, h], sem, sibling).wait_send()

    sums = []
    for n in range(2):
        for way in (0, 1):
            w_arrived(way, 7, 2 * n + way).wait_recv()
        add(n, (z + 8) % NZ)
        csrc[n] = acc[n, pl.ds(pl.multiple_of((1 - xlo) * T, T), T), :].astype(jnp.bfloat16)
        copy = remote(csrc.at[n], cbuf.at[n], cs.at[n], cr.at[n], partner)
        copy.start()
        sums.append(copy)
    for n, copy in enumerate(sums):
        copy.wait_recv()
        cols = pl.ds(n * WIDE, WIDE)
        mixed = acc[n, pl.ds(pl.multiple_of(xlo * T, T), T), :] + cbuf[n].astype(F32)
        out[:, cols] = (stream[:, cols].astype(F32) + mixed).astype(jnp.bfloat16)

    for copy in sums:
        copy.wait_send()
    for way, j, q in sent:
        if j == 7:
            w_copy(way, j, q).wait_send()


def shards(stream_in, features, conv_taps, decay, residues, state_in, out_weight):
    vmem = pl.BlockSpec(memory_space=pltpu.VMEM)
    hbm = pl.BlockSpec(memory_space=pl.ANY)
    D = Q * LANES
    dma = pltpu.SemaphoreType.DMA
    return pl.pallas_call(
        kernel,
        out_shape=jax.ShapeDtypeStruct((T, D), jnp.bfloat16),
        in_specs=[hbm] * 7,
        out_specs=vmem,
        scratch_shapes=[
            pltpu.VMEM((3, 3, D), F32),
            pltpu.VMEM((POLES, D), F32),
            pltpu.VMEM((POLES, D), F32),
            pltpu.VMEM((POLES, D), F32),
            pltpu.VMEM((T, D), jnp.bfloat16),
            pltpu.VMEM((2, NZ, WIDE, WIDE), jnp.bfloat16),
            pltpu.VMEM((3, NZ, T, 2 * LANES), jnp.bfloat16),
            pltpu.VMEM((2, T, 2 * LANES), jnp.bfloat16),
            pltpu.VMEM((3, T, D), jnp.bfloat16),
            pltpu.VMEM((3, T + 8, D), F32),
            pltpu.VMEM((8, D), F32),
            pltpu.VMEM((8, D), F32),
            pltpu.VMEM((Q, T, LANES), F32),
            pltpu.VMEM((Q, T, LANES), F32),
            pltpu.VMEM((Q, STEPS, SUB, LANES), F32),
            pltpu.VMEM((Q, POLES, SUB, LANES), F32),
            pltpu.VMEM((Q, T, LANES), F32),
            *[pltpu.VMEM((NZ, 2, LANES), F32)] * 6,
            *[pltpu.VMEM((2, LANES), F32)] * 3,
            pltpu.VMEM((Q, POLES, LANES), F32),
            pltpu.VMEM((2, 2 * T, WIDE), F32),
            pltpu.VMEM((2, T, WIDE), jnp.bfloat16),
            pltpu.VMEM((2, T, WIDE), jnp.bfloat16),
            dma((2, 8, Q)), dma((2, 8, Q)),
            dma((4, 2, 2)), dma((2, 8, 2)), dma((4, 2)), dma((4, 2)), dma((16,)),
            dma((NZ,)), dma((NZ,)), dma((NZ,)), dma((NZ,)), dma((2,)),
            dma((2,)), dma((2,)), dma((2,)), dma((Q + 6,)),
            pltpu.SemaphoreType.REGULAR((8,)),
        ],
        compiler_params=pltpu.CompilerParams(
            collective_id=0, has_side_effects=True, vmem_limit_bytes=60 * 2**20),
    )(features, conv_taps, decay.T, residues.T, state_in.T, stream_in, out_weight)


def solution(mesh):
    return jax.shard_map(
        shards,
        mesh=mesh,
        in_specs=(
            P("seq", "chan"),
            P(None, "seq", "chan"),
            P(None, None, "chan"),
            P("chan", None),
            P("chan", None),
            P("chan", None),
            P("seq", "chan"),
        ),
        out_specs=P("seq", "chan"),
        check_vma=False,
    )
```

```python
import jax
import jax.numpy as jnp
from jax import lax
from jax.experimental import pallas as pl
from jax.experimental.pallas import tpu as pltpu
from jax.sharding import PartitionSpec as P

FIRST, EACH = 4.2, 1.42
KNOW_AT = (2.5, 6.0, 9.5)
ENDS_AT, STARTS_AT = 17.5, 26.0
Y_AT = (30.5, 31.0, 32.0, 32.5, 33.5, 34.5)
X_AT = (34.5, 34.5, 34.5, 35.5, 35.5, 35.5, 37.0, 37.5, 38.0, 39.0, 40.0, 40.5)
SIBLING_AT = 44.0
DOT = 0.25

MESH = pl.DeviceIdType.MESH
F32 = jnp.float32
LANES = 128
WIDE = 256
Q = 4
POLES = 8
T = 128
SUB = 8
STEPS = T // SUB
NZ = 16
NS = 32


def place():
    s = lax.axis_index("seq")
    c = lax.axis_index("chan")
    return s, c, s // NZ, s % NZ, c // 4, (c // 2) % 2, c % 2


def kernel(feat, taps_h, dec_h, res_h, sin_h, stream_h, w, out,
           taps, dec, res, sin, stream, wbuf, gall, gown, fraw, fpad, tail, halo, pbuf, qbuf, ybuf, xs, gf, ends, ends_in, starts, starts_in, dec16, sin16, seed, total_out, total_in, sbuf, acc, csrc, cbuf,
           ws, wr, gs, gr, ys, sr, fs, es, er, ts, tr, ps, hs, cs, cr, ls, know):
    s, c, xlo, z, y, xhi, core = place()

    def dev(xl, zz, yy, xh, co):
        return {"seq": xl * NZ + zz, "chan": yy * 4 + xh * 2 + co}

    def remote(src, dst, ssem, rsem, to):
        return pltpu.make_async_remote_copy(
            src_ref=src, dst_ref=dst, send_sem=ssem, recv_sem=rsem, device_id=to, device_id_type=MESH)

    sibling = dev(xlo, z, y, xhi, 1 - core)
    partner = dev(1 - xlo, z, y, xhi, core)
    up = dev(xlo, (z + 1) % NZ, y, xhi, core)
    down = dev(xlo, (z + NZ - 1) % NZ, y, xhi, core)

    barrier = pltpu.get_barrier_semaphore()

    def greet(to):
        pl.semaphore_signal(barrier, inc=1, device_id=to, device_id_type=MESH)

    def along_x(dx):
        x = (xhi * 2 + xlo + dx) % 4
        return dev(x % 2, z, y, x // 2, core)

    def along_y(dy):
        return dev(xlo, z, (y + dy) % 4, xhi, core)

    def along_z(dz):
        return dev(xlo, (z + dz + NZ) % NZ, y, xhi, core)

    near = [up, down, {"seq": (s + 1) % NS, "chan": c}, {"seq": (s + NS - 1) % NS, "chan": c}, sibling,
            along_x(1), along_x(3), along_y(1), along_y(3)]
    for to in near:
        greet(to)

    def tell(n, to):
        pl.semaphore_signal(know.at[n], inc=1, device_id=to, device_id_type=MESH)

    def heard(n):
        pl.semaphore_wait(know.at[n], 1)

    load_f = pltpu.make_async_copy(feat, fraw, ls.at[Q])
    load_f.start()
    own_w = [pltpu.make_async_copy(w.at[:, pl.ds(n * WIDE, WIDE)], wbuf.at[n, z], ls.at[n]) for n in range(2)]
    for o in own_w:
        o.start()
    small = [pltpu.make_async_copy(a, b, ls.at[Q + 1 + n]) for n, (a, b) in enumerate(
        ((taps_h, taps), (dec_h, dec), (res_h, res), (sin_h, sin), (stream_h, stream)))]
    for o in small:
        o.start()

    load_f.wait()
    for i in range(3):
        fpad[i, pl.ds(8, T), :] = fraw[i].astype(F32)
        tail[pl.ds(2 * i, 2), :] = fpad[i, pl.ds(8 + T - 2, 2), :]
    tail[pl.ds(6, 2), :] = jnp.zeros((2, Q * LANES), F32)
    for o in own_w:
        o.wait()
    pl.semaphore_wait(barrier, len(near))
    send_halo = remote(tail, halo, hs.at[0], hs.at[1], {"seq": (s + 1) % NS, "chan": c})
    send_halo.start()
    tell(0, up)
    tell(1, down)
    tell(6, along_y(3))
    tell(7, along_x(3))

    def chunk(block, q):
        return wbuf.at[q // 2, block, pl.ds(q % 2 * LANES, LANES)]

    def w_copy(way, j, q):
        block = (z + NZ - j) % NZ if way == 0 else (z + j) % NZ
        return remote(chunk(block, q), chunk(block, q), ws.at[way, j, q], wr.at[way, j, q], up if way == 0 else down)

    def w_arrived(way, j, q):
        block = (z + NZ - j - 1) % NZ if way == 0 else (z + j + 1) % NZ
        return remote(chunk(block, q), chunk(block, q), ws.at[way, j, q], wr.at[way, j, q], up if way == 0 else down)

    sent = []

    def w_send(way, j, q):
        copy = w_copy(way, j, q)
        copy.start()
        sent.append((way, j, q))

    for q in range(Q):
        w_send(0, 0, q)
        w_send(1, 0, q)


    forwards = [(j, q) for j in range(1, 8) for q in range(Q)]

    def until(t):
        while forwards and FIRST + EACH * (4 * (forwards[0][0] - 1) + forwards[0][1]) <= t:
            j, q = forwards.pop(0)
            for way in (0, 1):
                w_arrived(way, j - 1, q).wait_recv()
                if j < 7 or q % 2 == way:
                    w_send(way, j, q)

    for o in small:
        o.wait()

    send_halo.wait_recv()
    heard(0)
    heard(1)
    tell(2, along_z(2))
    tell(3, along_z(-2))
    first = s > 0
    for i in range(3):
        fpad[i, pl.ds(6, 2), :] = jnp.where(first, halo[pl.ds(2 * i, 2), :], 0.0)

    def conv(q, carry):
        cols = pl.ds(pl.multiple_of(q * LANES, LANES), LANES)

        def short(i):
            total = taps[i, 0:1, cols] * fpad[i, pl.ds(8, T), cols]
            total = total + taps[i, 1:2, cols] * fpad[i, pl.ds(7, T), cols]
            return total + taps[i, 2:3, cols] * fpad[i, pl.ds(6, T), cols]

        pbuf[q] = short(1) * short(2)
        return carry

    def conv_q(q, carry):
        cols = pl.ds(pl.multiple_of(q * LANES, LANES), LANES)
        total = taps[0, 0:1, cols] * fpad[0, pl.ds(8, T), cols]
        total = total + taps[0, 1:2, cols] * fpad[0, pl.ds(7, T), cols]
        qbuf[q] = total + taps[0, 2:3, cols] * fpad[0, pl.ds(6, T), cols]
        return carry

    lax.fori_loop(0, Q, conv, 0)

    row = lax.broadcasted_iota(jnp.int32, (SUB, LANES), 0)

    def inner(q, carry):
        cols = pl.ds(pl.multiple_of(q * LANES, LANES), LANES)
        rates = [jnp.broadcast_to(dec[r:r + 1, cols], (SUB, LANES)) for r in range(POLES)]
        step = [jnp.exp(-v) for v in rates]
        gain = [jnp.broadcast_to(res[r:r + 1, cols], (SUB, LANES)) for r in range(POLES)]
        x = [jnp.zeros((SUB, LANES), F32) for _ in range(POLES)]
        for j in range(STEPS):
            p = pbuf[q, pl.ds(j, SUB, stride=STEPS), :]
            x = [step[r] * x[r] + p for r in range(POLES)]
            ybuf[q, j] = sum(gain[r] * x[r] for r in range(POLES))
        for r in range(POLES):
            total = step[r] * x[r]
            for d in (1, 2, 4):
                moved = jnp.where(row >= d, pltpu.roll(total, d, 0), 0.0)
                total = total + jnp.exp(rates[r] * (-1.0 * STEPS * d)) * moved
            xs[q, r] = jnp.where(row >= 1, pltpu.roll(total, 1, 0), 0.0)
            ends[q * 4 + r // 2, r % 2:r % 2 + 1, :] = total[SUB - 1:SUB, :]
        return carry

    lax.fori_loop(0, Q, inner, 0)

    for q in range(Q):
        for p in range(4):
            part = (slice(2 * p, 2 * p + 2), slice(q * LANES, (q + 1) * LANES))
            dec16[q * 4 + p] = dec[part]
            sin16[q * 4 + p] = sin[part]

    def end_copy(n):
        to = (z + n) % NZ
        return remote(ends.at[to], ends_in.at[z], es.at[n], er.at[z], along_z(n))

    def end_arrives(n):
        came = (z + n) % NZ
        return remote(ends.at[0], ends_in.at[came], es.at[n], er.at[came], up)

    def start_copy(n):
        to = (z + n) % NZ
        return remote(starts.at[to], starts_in.at[z], ts.at[n], tr.at[z], along_z(n))

    def start_arrives(n):
        came = (z + n) % NZ
        return remote(starts.at[0], starts_in.at[came], ts.at[n], tr.at[came], up)

    def each(lo, hi, do):
        def step(n, carry):
            do(n)
            return carry

        lax.fori_loop(lo, hi, step, 0)

    heard(2)
    heard(3)
    tell(4, along_z(4))
    tell(5, along_z(-4))
    each(1, 5, lambda n: end_copy(n).start())
    each(12, 16, lambda n: end_copy(n).start())
    until(KNOW_AT[1])
    ends_in[z] = ends[z]
    until(KNOW_AT[2])
    heard(4)
    heard(5)
    each(5, 12, lambda n: end_copy(n).start())
    lax.fori_loop(0, Q, conv_q, 0)
    until(ENDS_AT)
    each(1, 16, lambda n: end_arrives(n).wait_recv())
    rate = jnp.exp(dec16[z] * (-1.0 * T))
    give_total = remote(total_out, total_in, ps.at[0], ps.at[1], partner)

    @pl.when(xlo == 0)
    def _():
        seed[...] = sin16[z]

    @pl.when(xlo == 1)
    def _():
        give_total.wait_recv()
        seed[...] = total_in[...]

    state = seed[...]
    for n in range(NZ):
        starts[n] = state
        state = rate * state + ends_in[n]

    @pl.when(xlo == 0)
    def _():
        total_out[...] = state
        give_total.start()

    each(1, 16, lambda n: start_copy(n).start())
    starts_in[z] = starts[z]
    until(STARTS_AT)
    each(1, 16, lambda n: start_arrives(n).wait_recv())
    for q in range(Q):
        for p in range(4):
            sbuf[q, 2 * p:2 * p + 2, :] = starts_in[q * 4 + p]

    def gate(q, carry):
        cols = pl.ds(pl.multiple_of(q * LANES, LANES), LANES)
        rates = [jnp.broadcast_to(dec[r:r + 1, cols], (SUB, LANES)) for r in range(POLES)]
        step = [jnp.exp(-v) for v in rates]
        back = row.astype(F32) * (-1.0 * STEPS)
        x = []
        for r in range(POLES):
            start = xs[q, r] + jnp.exp(rates[r] * back) * sbuf[q, r:r + 1, :]
            x.append(res[r:r + 1, cols] * start)
        for j in range(STEPS):
            total = ybuf[q, j] + sum(x)
            x = [step[r] * x[r] for r in range(POLES)]
            rows = pl.ds(j, SUB, stride=STEPS)
            gf[q, rows, :] = total * qbuf[q, rows, :]
        gown[q // 2, :, pl.ds(pl.multiple_of((q % 2) * LANES, LANES), LANES)] = gf[q].astype(jnp.bfloat16)
        return carry

    def spot(yy, h):
        other = (yy // 2 + xlo) % 2
        k = ((yy % 2) * 4 + xhi * 2 + core) * (1 - other) + (yy % 2) * other
        return gall.at[xlo * (1 - other) + 2 * other, 2 * k + h]

    def landing(yy, h):
        k = (yy % 2) * 4 + xhi * 2 + core
        return gall.at[xlo, 2 * k + h], gr.at[xlo, k, h]

    def send_x(n, h, src):
        yy = (y + n) % 4
        dst, sem = landing(yy, h)
        same = yy // 2 == xlo

        @pl.when(same)
        def _():
            remote(src, dst, gs.at[n, 0, h], sem, along_x(2)).start()

        @pl.when(jnp.logical_not(same))
        def _():
            remote(src, dst, gs.at[n, 0, h], sem, along_x(1)).start()
            remote(src, dst, gs.at[n, 1, h], sem, along_x(3)).start()

    heard(6)
    heard(7)
    home = y // 2 == xlo
    y_sends = []
    for h in range(2):
        lax.fori_loop(2 * h, 2 * h + 2, gate, 0)

        @pl.when(home)
        def _():
            pltpu.make_async_copy(gown.at[h], spot(y, h), sr.at[y, h]).start()

        for n in (1, 3, 2):
            copy = remote(gown.at[h], spot(y, h), ys.at[n, h], sr.at[y, h], along_y(n))
            copy.start()
            y_sends.append(copy)
        send_x(0, h, gown.at[h])
    passed = []

    def to_sibling(slot, sem):
        copy = remote(slot, slot, fs.at[len(passed)], sem, sibling)
        copy.start()
        passed.append((slot, sem))

    for i, (n, h) in enumerate(((1, 0), (3, 0), (1, 1), (3, 1), (2, 0), (2, 1))):
        until(Y_AT[i])
        yy = (y + n) % 4
        remote(spot(yy, h), spot(yy, h), ys.at[n, h], sr.at[yy, h], sibling).wait_recv()
        send_x(n, h, spot(yy, h))

    def arrived(xl, yy, xh, co, h):
        k = yy * 4 + xh * 2 + co
        return gall.at[xl, 2 * k + h], gr.at[xl, k, h]

    @pl.when(home)
    def _():
        for h in range(2):
            pltpu.make_async_copy(gown.at[h], spot(y, h), sr.at[y, h]).wait()

    for yy in range(2):
        for h in range(2):
            to_sibling(*arrived(xlo, yy, xhi, core, h))
    nearer = (y + y // 2 + xlo) % 2
    for i in range(2):
        yy = (nearer + i) % 2
        for h in range(2):
            for xl, xh in ((1 - xlo, xhi), (1 - xlo, 1 - xhi), (xlo, 1 - xhi)):
                until(X_AT[len(passed) - 4])
                slot, sem = arrived(xl, yy, xh, core, h)
                remote(slot, slot, fs.at[0], sem, sibling).wait_recv()
                to_sibling(slot, sem)
    until(SIBLING_AT)
    for xl in range(2):
        for yy in range(2):
            for xh in range(2):
                for h in range(2):
                    slot, sem = arrived(xl, yy, xh, 1 - core, h)
                    remote(slot, slot, fs.at[0], sem, sibling).wait_recv()

    def add(n, block, fresh=False):
        lhs = gall[pl.ds(0, 2), block].reshape(2 * T, WIDE)
        part = jnp.dot(lhs, wbuf[n, block], preferred_element_type=F32)
        acc[n] = part if fresh else acc[n] + part

    clock = SIBLING_AT
    for n in range(2):
        add(n, z, fresh=True)
    for i in range(1, 8):
        for block in ((z + i) % NZ, (z + NZ - i) % NZ):
            clock += DOT
            until(clock)
            while forwards and forwards[0][0] <= i:
                until(FIRST + EACH * (4 * (forwards[0][0] - 1) + forwards[0][1]))
            for n in range(2):
                add(n, block)
    for n, (slot, sem) in enumerate(passed):
        remote(slot, slot, fs.at[n], sem, sibling).wait_send()
    each(1, 16, lambda n: end_copy(n).wait_send())
    each(1, 16, lambda n: start_copy(n).wait_send())

    @pl.when(xlo == 0)
    def _():
        give_total.wait_send()

    send_halo.wait_send()
    for way, j, q in sent:
        if j < 7:
            w_copy(way, j, q).wait_send()
    for copy in y_sends:
        copy.wait_send()
    for n in range(4):
        for h in range(2):
            dst, sem = landing((y + n) % 4, h)
            remote(gown.at[h], dst, gs.at[n, 0, h], sem, sibling).wait_send()

            @pl.when((y + n) % 4 // 2 != xlo)
            def _():
                remote(gown.at[h], dst, gs.at[n, 1, h], sem, sibling).wait_send()

    sums = []
    for n in range(2):
        for way in (0, 1):
            w_arrived(way, 7, 2 * n + way).wait_recv()
        far = (z + 8) % NZ
        theirs = pl.ds(pl.multiple_of((1 - xlo) * T, T), T)
        last = jnp.dot(gall[1 - xlo, far], wbuf[n, far], preferred_element_type=F32)
        csrc[n] = (acc[n, theirs, :] + last).astype(jnp.bfloat16)
        copy = remote(csrc.at[n], cbuf.at[n], cs.at[n], cr.at[n], partner)
        copy.start()
        sums.append(copy)
    for n, copy in enumerate(sums):
        cols = pl.ds(n * WIDE, WIDE)
        far = (z + 8) % NZ
        mixed = acc[n, pl.ds(pl.multiple_of(xlo * T, T), T), :] + stream[:, cols].astype(F32)
        mixed = mixed + jnp.dot(gall[xlo, far], wbuf[n, far], preferred_element_type=F32)
        copy.wait_recv()
        out[:, cols] = (mixed + cbuf[n].astype(F32)).astype(jnp.bfloat16)

    for copy in sums:
        copy.wait_send()
    for way, j, q in sent:
        if j == 7:
            w_copy(way, j, q).wait_send()


def shards(stream_in, features, conv_taps, decay, residues, state_in, out_weight):
    vmem = pl.BlockSpec(memory_space=pltpu.VMEM)
    hbm = pl.BlockSpec(memory_space=pl.ANY)
    D = Q * LANES
    dma = pltpu.SemaphoreType.DMA
    return pl.pallas_call(
        kernel,
        out_shape=jax.ShapeDtypeStruct((T, D), jnp.bfloat16),
        in_specs=[hbm] * 7,
        out_specs=vmem,
        scratch_shapes=[
            pltpu.VMEM((3, 3, D), F32),
            pltpu.VMEM((POLES, D), F32),
            pltpu.VMEM((POLES, D), F32),
            pltpu.VMEM((POLES, D), F32),
            pltpu.VMEM((T, D), jnp.bfloat16),
            pltpu.VMEM((2, NZ, WIDE, WIDE), jnp.bfloat16),
            pltpu.VMEM((3, NZ, T, 2 * LANES), jnp.bfloat16),
            pltpu.VMEM((2, T, 2 * LANES), jnp.bfloat16),
            pltpu.VMEM((3, T, D), jnp.bfloat16),
            pltpu.VMEM((3, T + 8, D), F32),
            pltpu.VMEM((8, D), F32),
            pltpu.VMEM((8, D), F32),
            pltpu.VMEM((Q, T, LANES), F32),
            pltpu.VMEM((Q, T, LANES), F32),
            pltpu.VMEM((Q, STEPS, SUB, LANES), F32),
            pltpu.VMEM((Q, POLES, SUB, LANES), F32),
            pltpu.VMEM((Q, T, LANES), F32),
            *[pltpu.VMEM((NZ, 2, LANES), F32)] * 6,
            *[pltpu.VMEM((2, LANES), F32)] * 3,
            pltpu.VMEM((Q, POLES, LANES), F32),
            pltpu.VMEM((2, 2 * T, WIDE), F32),
            pltpu.VMEM((2, T, WIDE), jnp.bfloat16),
            pltpu.VMEM((2, T, WIDE), jnp.bfloat16),
            dma((2, 8, Q)), dma((2, 8, Q)),
            dma((4, 2, 2)), dma((2, 8, 2)), dma((4, 2)), dma((4, 2)), dma((16,)),
            dma((NZ,)), dma((NZ,)), dma((NZ,)), dma((NZ,)), dma((2,)),
            dma((2,)), dma((2,)), dma((2,)), dma((Q + 6,)),
            pltpu.SemaphoreType.REGULAR((8,)),
        ],
        compiler_params=pltpu.CompilerParams(
            collective_id=0, has_side_effects=True, vmem_limit_bytes=60 * 2**20),
    )(features, conv_taps, decay.T, residues.T, state_in.T, stream_in, out_weight)


def solution(mesh):
    return jax.shard_map(
        shards,
        mesh=mesh,
        in_specs=(
            P("seq", "chan"),
            P(None, "seq", "chan"),
            P(None, None, "chan"),
            P("chan", None),
            P("chan", None),
            P("chan", None),
            P("seq", "chan"),
        ),
        out_specs=P("seq", "chan"),
        check_vma=False,
    )
```
